32 devices in a mesh: row: 4 (over y, x), col: 8 (over z, core).
Axes of the slice: x: 2, y: 2, z: 4, core: 2. Of those that a mesh axis runs over, the one named last changes fastest.
Arguments:
- positions: float32 [3, 4096, 128], P(None, ('row', 'col')), may hold values from -6 to 6
- block_links: int32 [2, 4096], replicated, may hold values from 0 to 4095, as said below
- panel_points: int32 [4, 256], replicated, may hold values from 0 to 524287
Outputs:
- smoothed: float32 [3, 8192, 128], P(None, ('row', 'col'))
- velocity: float32 [4, 3, 256], P('row', None, 'col')
The draws below stay inside these ranges and needn't reach their ends.
Inputs may be any that keep to these rules, and one draw needn't show every extreme that they name: block_links[0, b] is an owner device, numbered in the order of row+col; block_links[1] is a permutation of the 4096 blocks whose cycles are the loops, and all blocks of one loop have one owner. The 128 blocks of one device, b // 128, include at most 8 of any one owner, and in every draw one owner has exactly 8 blocks on every device.
All inputs are finite; a program needn't handle non-finite values.
Results may differ from the reference program's by a relative error of at most 0.0003.
Values sent between devices are 32-bit elements; how exact they have to be, the bound alone decides.
No kernel may reach another device: no remote copies, remote signals or barrier semaphores. Data moves between devices by JAX's collectives and lax.ppermute only.
A program may use at most 128 MiB of HBM per device.

```python
import math
import jax
import jax.numpy as jnp
from jax import lax

BLK = 128
PANEL = 256
SWEEPS = 2
SLOT_DEV = 128
CAP = 8
NSTORE = 4096
NOWN = 8192
POINTS = 524288
N_ROW = 4
DEVICES = 32


def loop_tables(key):
    key_busy, key_owner, key_order, key_break = jax.random.split(jax.random.fold_in(key, 11), 4)
    busiest = jax.random.randint(key_busy, (), 0, DEVICES, dtype=jnp.int32)
    others = jnp.arange(DEVICES - 1, dtype=jnp.int32)
    others = others + (others >= busiest).astype(jnp.int32)
    spares = jnp.repeat(others, CAP)

    def one_device(dev_key):
        key_remain, key_mix = jax.random.split(dev_key)
        remain = jax.random.permutation(key_remain, spares)[:SLOT_DEV - CAP]
        chosen = jnp.concatenate([jnp.full((CAP,), busiest, jnp.int32), remain])
        return jax.random.permutation(key_mix, chosen)
    owners = jax.vmap(one_device)(jax.random.split(key_owner, DEVICES)).reshape(NSTORE).astype(jnp.int32)
    shuffle = jax.random.permutation(key_order, NSTORE).astype(jnp.int32)
    orders = jnp.argsort(owners * NSTORE + shuffle).astype(jnp.int32)
    sorted_owner = owners[orders]
    indices = jnp.arange(NSTORE, dtype=jnp.int32)
    breaks = jax.random.randint(key_break, (NSTORE,), 0, 4) != 0
    change = jnp.concatenate([jnp.ones((1,), bool), sorted_owner[1:] != sorted_owner[:-1]])
    begins = jnp.logical_or(breaks, change)
    starts = lax.cummax(jnp.where(begins, indices, 0), axis=0)
    starts_at = jnp.where(begins, indices, NSTORE).astype(jnp.int32)
    following = lax.cummin(jnp.concatenate([starts_at[1:], jnp.full((1,), NSTORE, jnp.int32)]), axis=0, reverse=True)
    finish = following - 1
    step_to = jnp.where(indices < finish, indices + 1, starts)
    follows = jnp.zeros((NSTORE,), jnp.int32).at[orders].set(orders[step_to])
    return jnp.stack([owners, follows])


def draw_block_links(key, part):
    return loop_tables(key)


def with_ends(entries, key, least, top_value):
    place = [jax.random.randint(jax.random.fold_in(key, axis), (), 0, length) for axis, length in enumerate(entries.shape)]
    widest = entries.shape.index(max(entries.shape))
    neighbour = place[:widest] + [(place[widest] + 1) % entries.shape[widest]] + place[widest + 1:]
    return entries.at[tuple(place)].set(least).at[tuple(neighbour)].set(top_value)


def block_levels(rng, dims, shards, least, top_value):
    level = 1.0
    for dim, blocks in shards:
        draws = jax.random.uniform(jax.random.fold_in(jax.random.fold_in(rng, 6), dim), (blocks,), jnp.float32, least / len(shards), top_value / len(shards))
        level = level * jnp.repeat(jnp.exp(draws), dims[dim] // blocks).reshape((-1,) + (1,) * (len(dims) - 1 - dim))
    return level


def centred(rng, extent, deviation, bound, cuts=(), kind=jnp.bfloat16):
    factor_of = block_levels(rng, extent, cuts, -0.22, 0.18) if cuts else 1.0
    values = jax.random.normal(rng, extent, jnp.float32) * deviation * factor_of
    return jnp.minimum(jnp.maximum(values, -bound), bound).astype(kind)


def setup_inputs(seed: int = 0) -> dict:
    streams_of = jax.random.split(jax.random.key(seed), 4)
    return {
        "positions": centred(streams_of[0], (3, NSTORE, BLK), 1.0, 6.0, ((1, 32),), jnp.float32),
        "block_links": draw_block_links(jax.random.fold_in(streams_of[3], 71), 0),
        "panel_points": with_ends(jax.random.randint(streams_of[2], (N_ROW, PANEL), 0, POINTS), jax.random.fold_in(streams_of[2], 1), 0, POINTS - 1).astype(jnp.int32),
    }


SMOOTH_RATE = 0.25
CORE_SQUARED = 0.01

def cross_three(left_vec, right_vec):
    return jnp.stack([left_vec[1] * right_vec[2] - left_vec[2] * right_vec[1], left_vec[2] * right_vec[0] - left_vec[0] * right_vec[2], left_vec[0] * right_vec[1] - left_vec[1] * right_vec[0]])

def neighbours(points, next_block, prev_block):
    ahead = jnp.concatenate([points[:, :, 1:], points[:, next_block, :1]], axis=2)
    behind = jnp.concatenate([points[:, prev_block, -1:], points[:, :, :-1]], axis=2)
    return (behind, ahead)

def smooth_loops(points, next_block, prev_block):
    for sweep_no in range(SWEEPS):
        behind, ahead = neighbours(points, next_block, prev_block)
        points = points + SMOOTH_RATE * (behind - 2.0 * points + ahead)
    return points

def panel_sums(targets, sources):
    centres = sources[:3]
    segments = sources[3:]
    inner = lax.dot_general(targets, centres, (((0,), (0,)), ((), ())), precision=lax.Precision.HIGHEST)
    squared = lax.optimization_barrier(jnp.sum(targets * targets, 0))[:, None] + lax.optimization_barrier(jnp.sum(centres * centres, 0))[None, :] - 2.0 * inner + CORE_SQUARED
    weights = 1.0 / (squared * jnp.sqrt(squared))
    features = jnp.concatenate([segments, cross_three(segments, centres)], 0)
    return lax.dot_general(weights, features, (((1,), (1,)), ((), ())), precision=lax.Precision.HIGHEST)

def reference(positions, block_links, panel_points):
    owners = block_links[0]
    follows = block_links[1]
    counter = jnp.arange(NSTORE, dtype=jnp.int32)
    precedes = jnp.zeros_like(follows).at[follows].set(counter)
    smoothed = smooth_loops(positions, follows, precedes)
    owner_grid = owners.reshape(DEVICES, SLOT_DEV)
    same_owner = owner_grid[:, :, None] == owner_grid[:, None, :]
    earlier = jnp.arange(SLOT_DEV)[None, :] < jnp.arange(SLOT_DEV)[:, None]
    ranks = lax.optimization_barrier(jnp.sum(jnp.logical_and(same_owner, earlier[None]), axis=2)).astype(jnp.int32).reshape(NSTORE)
    places = owners * (DEVICES * CAP) + counter // SLOT_DEV * CAP + ranks
    layout = jnp.zeros((3, NOWN, BLK), jnp.float32).at[:, places, :].set(smoothed)
    behind, ahead = neighbours(smoothed, follows, precedes)
    segments = ahead - smoothed
    centres = 0.5 * (ahead + smoothed)
    wanted = panel_points.reshape(-1)
    targets = smoothed[:, wanted // BLK, wanted % BLK]
    tiles = NSTORE // 128
    sources = jnp.concatenate([centres, segments], 0).reshape(6, tiles, 128 * BLK)
    sources = jnp.moveaxis(sources, 1, 0)

    def add_tile(running, tile):
        return (running + panel_sums(targets, tile), None)
    sums, unused = lax.scan(add_tile, jnp.zeros((wanted.shape[0], 6), jnp.float32), sources)
    scale = 1.0 / (math.pi * math.sqrt(NSTORE * BLK))
    velocity = scale * (cross_three(sums[:, :3].T, targets) - sums[:, 3:].T)
    velocity = jnp.transpose(velocity.reshape(3, N_ROW, PANEL), (1, 0, 2))
    return (layout, velocity)
```

```python
import functools
import math

import jax
import jax.numpy as jnp
from jax import lax
from jax.experimental import pallas as pl
from jax.experimental.pallas import tpu as pltpu
from jax.sharding import PartitionSpec as P

CORE_SQUARED = 0.01
F32 = jnp.float32
BF16 = jnp.bfloat16
LANES = 128
DEPTH = 32
FEATS = 16
EDGES = 5
AXES = ("row", "col")


def iota(shape, dim):
    return lax.broadcasted_iota(jnp.int32, shape, dim)


def three_parts(value):
    first = value.astype(BF16)
    rest = value - first.astype(F32)
    second = rest.astype(BF16)
    third = (rest - second.astype(F32)).astype(BF16)
    return (first, second, third)


def dot(left, right):
    return jnp.dot(left, right, preferred_element_type=F32)


def pick(onehot, value):
    first, second, third = three_parts(value)
    return dot(onehot, first) + dot(onehot, second) + dot(onehot, third)


def as_columns(row):
    return jnp.transpose(jnp.broadcast_to(row.astype(F32), (LANES, row.shape[1])))


def shifted(value, steps):
    return pltpu.roll(value, (-steps) % LANES, 1)


def five_taps(far_left, left, here, right, far_right):
    return (far_left + far_right + 4.0 * (left + right) + 6.0 * here) * 0.0625


def cross(left_vec, right_vec):
    return [
        left_vec[1] * right_vec[2] - left_vec[2] * right_vec[1],
        left_vec[2] * right_vec[0] - left_vec[0] * right_vec[2],
        left_vec[0] * right_vec[1] - left_vec[1] * right_vec[0],
    ]


def source_rows(here, ahead, keep=None):
    segment = [a - h for a, h in zip(ahead, here)]
    centre = [0.5 * (a + h) for a, h in zip(ahead, here)]
    if keep is not None:
        segment = [jnp.where(keep, s, 0.0) for s in segment]
    near = []
    for value in centre:
        one, two, three = [part.astype(F32) for part in three_parts(value)]
        near += [one, two, three, one, two, one]
    norm = centre[0] * centre[0] + centre[1] * centre[1] + centre[2] * centre[2]
    near += [part.astype(F32) for part in three_parts(norm)]
    near += [jnp.ones_like(norm)] * 3
    terms = segment + cross(segment, centre)
    tops = [value.astype(BF16).astype(F32) for value in terms]
    sums = tops + [value - top for value, top in zip(terms, tops)]
    return near, sums


def target_rows(targets):
    rows = []
    for value in targets:
        one, two, three = [part.astype(F32) for part in three_parts(-2.0 * value)]
        rows += [one, one, one, two, two, three]
    norm = targets[0] * targets[0] + targets[1] * targets[1] + targets[2] * targets[2]
    rows += [jnp.ones_like(norm)] * 3
    rows += [part.astype(F32) for part in three_parts(norm + CORE_SQUARED)]
    return rows


def pair_sums(near, sums, target_side):
    squared = lax.dot_general(
        near, target_side, (((0,), (0,)), ((), ())), preferred_element_type=F32
    )
    root = lax.rsqrt(squared)
    weight = root * root * root
    top = weight.astype(BF16)
    rest = (weight - top.astype(F32)).astype(BF16)
    return dot(sums, top) + dot(sums, rest)


def prep_kernel(cap, me_ref, pos_ref, links_ref, panel_ref, part_ref, out_ref, near_ref, sums_ref, near_scr, sums_scr):
    me = me_ref[0]
    blocks = pos_ref.shape[1]
    held = out_ref.shape[1]
    total = links_ref.shape[1]
    copies = part_ref.shape[0]
    base = me * blocks
    mine = pl.ds(pl.multiple_of(base, LANES), blocks)
    lane = iota((blocks, LANES), 1)
    ids = iota((blocks, LANES), 0) + base

    wanted = jnp.concatenate([panel_ref[r : r + 1, :] for r in range(panel_ref.shape[0])], axis=1)
    count = wanted.shape[1]
    shift = LANES.bit_length() - 1
    wanted_block = lax.shift_right_logical(wanted, shift)
    wanted_point = jnp.bitwise_and(wanted, LANES - 1)

    follow_col = as_columns(links_ref[1:2, mine]).astype(jnp.int32)[:, :1]
    found = jnp.zeros((blocks, LANES), F32)
    lane_f = lane.astype(F32)
    for r in range(total // LANES):
        row = links_ref[1:2, r * LANES : (r + 1) * LANES]
        found = found + jnp.where(row == ids, lane_f + float(r * LANES), 0.0)
    precede_col = jnp.sum(found, axis=1, keepdims=True).astype(jnp.int32)

    held_here = wanted_block == (iota((blocks, count), 0) + base)
    before = jnp.logical_and(wanted_point < 2, follow_col == wanted_block)
    after = jnp.logical_and(wanted_point >= LANES - 2, precede_col == wanted_block)
    onehot = jnp.concatenate(
        [
            jnp.where(held_here, 1.0, 0.0).astype(BF16),
            jnp.where(jnp.logical_or(before, after), 1.0, 0.0).astype(BF16),
        ],
        axis=0,
    )
    at_point = iota((LANES, count), 0) == wanted_point

    here_all = []
    for c in range(3):
        x = pos_ref[c]
        rolled = {s: shifted(x, s) for s in (-2, -1, 1, 2)}
        inner = {
            s: jnp.where((lane >= -s) if s < 0 else (lane < LANES - s), v, 0.0)
            for s, v in rolled.items()
        }
        outer = {s: rolled[s] - inner[s] for s in rolled}
        own = five_taps(inner[-2], inner[-1], x, inner[1], inner[2])
        other = five_taps(outer[-2], outer[-1], 0.0, outer[1], outer[2])
        here_all.append(own)
        both = jnp.transpose(jnp.concatenate([own, other], axis=0))
        one, two, three = three_parts(both)
        values = dot(one, onehot) + dot(two, onehot) + dot(three, onehot)
        row = jnp.sum(jnp.where(at_point, values, 0.0), axis=0, keepdims=True)
        per = count // LANES
        for i in range(per):
            part_ref[:, c * per + i, :] = jnp.broadcast_to(
                row[:, i * LANES : (i + 1) * LANES], (copies, LANES)
            )

    owner_row = links_ref[0:1, mine]
    owner_col = as_columns(owner_row).astype(jnp.int32)
    same = jnp.logical_and(owner_col == owner_row, iota((blocks, blocks), 0) < iota((blocks, blocks), 1))
    rank = jnp.sum(jnp.where(same, 1.0, 0.0), axis=0, keepdims=True).astype(jnp.int32)
    slot = owner_row * cap + rank
    into = jnp.where(iota((held, blocks), 0) == slot, 1.0, 0.0).astype(BF16)
    for c in range(3):
        out_ref[c] = pick(into, pos_ref[c])

    ahead_all = [shifted(v, 1) for v in here_all]
    keep = jnp.logical_and(lane >= 2, lane <= LANES - 4)
    near, sums = source_rows(here_all, ahead_all, keep)
    near_scr[...] = jnp.zeros_like(near_scr)
    sums_scr[...] = jnp.zeros_like(sums_scr)
    for k, value in enumerate(near):
        near_scr[pl.ds(k, blocks, stride=DEPTH), :] = value
    for k, value in enumerate(sums):
        sums_scr[pl.ds(k, blocks, stride=FEATS), :] = value
    for b in range(blocks):
        near_ref[:, b * LANES : (b + 1) * LANES] = near_scr[b * DEPTH : (b + 1) * DEPTH, :].astype(BF16)
        sums_ref[:, b * LANES : (b + 1) * LANES] = sums_scr[b * FEATS : (b + 1) * FEATS, :].astype(BF16)


def pair_kernel(tile, parts, part_ref, near_ref, sums_ref, acc_ref, side_ref, target_ref, rows_scr):
    added = jnp.sum(part_ref[...], axis=0)
    per = added.shape[0] // 3
    targets = [
        jnp.concatenate([added[c * per + i : c * per + i + 1, :] for i in range(per)], axis=1)
        for c in range(3)
    ]
    rows_scr[...] = jnp.zeros_like(rows_scr)
    for c in range(3):
        target_ref[c : c + 1, :] = targets[c]
    for k, row in enumerate(target_rows(targets)):
        rows_scr[k : k + 1, :] = row
    side_ref[...] = rows_scr[...].astype(BF16)
    count = side_ref.shape[1]
    piece = tile // parts

    def one_tile(turn, running):
        result = []
        for s in range(parts):
            at = pl.ds(pl.multiple_of(turn * tile + s * piece, piece), piece)
            result.append(running[s] + pair_sums(near_ref[:, at], sums_ref[:, at], side_ref[...]))
        return tuple(result)

    zeros = tuple(jnp.zeros((FEATS, count), F32) for s in range(parts))
    running = lax.fori_loop(0, near_ref.shape[1] // tile, one_tile, zeros)
    acc_ref[...] = sum(running[1:], running[0])


def owner_kernel(cap, scale, me_ref, links_ref, arrived_ref, side_ref, target_ref, acc_ref, smooth_ref, vel_ref, owner_scr, follow_scr, near_scr, sums_scr):
    me = me_ref[0]
    held = arrived_ref.shape[1]
    devices = owner_scr.shape[0]
    for r in range(devices):
        owner_scr[r : r + 1, :] = links_ref[0:1, r * LANES : (r + 1) * LANES]
        follow_scr[r : r + 1, :] = links_ref[1:2, r * LANES : (r + 1) * LANES]
    owned = jnp.where(owner_scr[...] == me, 1.0, 0.0)
    upper = jnp.where(iota((LANES, LANES), 0) < iota((LANES, LANES), 1), 1.0, 0.0)
    rank = dot(owned.astype(BF16), upper.astype(BF16))
    shift = LANES.bit_length() - 1
    follow = follow_scr[...]
    table = jnp.concatenate(
        [
            owned,
            rank,
            lax.shift_right_logical(follow, shift).astype(F32),
            jnp.bitwise_and(follow, LANES - 1).astype(F32),
        ],
        axis=1,
    ).astype(BF16)
    cap_shift = cap.bit_length() - 1
    slot = iota((held, devices), 0)
    spread = jnp.where(
        lax.shift_right_logical(slot, cap_shift) == iota((held, devices), 1), 1.0, 0.0
    ).astype(BF16)
    wide = dot(spread, table)
    slots = iota((held, LANES), 0)
    seat = jnp.bitwise_and(slots, cap - 1).astype(F32)
    hit = jnp.logical_and(wide[:, :LANES] == 1.0, wide[:, LANES : 2 * LANES] == seat)
    number = (lax.shift_right_logical(slots, cap_shift) * LANES + iota((held, LANES), 1)).astype(F32)
    target_no = wide[:, 2 * LANES : 3 * LANES] * float(LANES) + wide[:, 3 * LANES :]
    live = jnp.sum(jnp.where(hit, 1.0, 0.0), axis=1, keepdims=True)
    id_col = jnp.sum(jnp.where(hit, number, 0.0), axis=1, keepdims=True) + live - 1.0
    next_col = jnp.sum(jnp.where(hit, target_no, 0.0), axis=1, keepdims=True) + 2.0 * live - 2.0
    id_row = jnp.transpose(jnp.broadcast_to(id_col, (held, LANES)))[:1, :]
    next_row = jnp.transpose(jnp.broadcast_to(next_col, (held, LANES)))[:1, :]
    to_next = jnp.where(next_col == id_row, 1.0, 0.0).astype(BF16)
    to_prev = jnp.where(id_col == next_row, 1.0, 0.0).astype(BF16)

    lane = iota((held, LANES), 1)
    here_rows = []
    ahead_rows = []
    for c in range(3):
        x = arrived_ref[c]
        after = pick(to_next, x)
        before = pick(to_prev, x)
        at = {0: x}
        for s in (-2, -1):
            at[s] = jnp.where(lane < -s, shifted(before, s), shifted(x, s))
        for s in (1, 2, 3):
            at[s] = jnp.where(lane >= LANES - s, shifted(after, s), shifted(x, s))
        y = five_taps(at[-2], at[-1], at[0], at[1], at[2])
        smooth_ref[c] = y
        ahead = five_taps(at[-1], at[0], at[1], at[2], at[3])
        y_t = jnp.transpose(y)
        ahead_t = jnp.transpose(ahead)
        here_rows.append(jnp.concatenate([y_t[:2], y_t[LANES - 3 :]], axis=0))
        ahead_rows.append(jnp.concatenate([ahead_t[:2], ahead_t[LANES - 3 :]], axis=0))
    near, sums = source_rows(here_rows, ahead_rows)
    near_scr[...] = jnp.zeros_like(near_scr)
    sums_scr[...] = jnp.zeros_like(sums_scr)
    for k, value in enumerate(near):
        for e in range(EDGES):
            near_scr[k : k + 1, e * held : (e + 1) * held] = value[e : e + 1, :]
    for k, value in enumerate(sums):
        for e in range(EDGES):
            sums_scr[k : k + 1, e * held : (e + 1) * held] = value[e : e + 1, :]
    acc = acc_ref[...] + pair_sums(near_scr[...].astype(BF16), sums_scr[...].astype(BF16), side_ref[...])
    terms = acc[0:6] + acc[6:12]
    targets = [target_ref[c : c + 1, :] for c in range(3)]
    turned = cross([terms[c : c + 1, :] for c in range(3)], targets)
    for c in range(3):
        vel_ref[c : c + 1, :] = scale * (turned[c] - terms[3 + c : 4 + c, :])


def shards(positions, block_links, panel_points):
    devices = lax.axis_size(AXES)
    me = lax.axis_index(AXES).astype(jnp.int32).reshape(1)
    blocks = positions.shape[1]
    cap = 2 * blocks // devices
    held = devices * cap
    total = block_links.shape[1]
    points = blocks * LANES
    panel = panel_points.shape[1]
    count = panel_points.shape[0] * panel
    share = panel // lax.axis_size("col")
    scale = 1.0 / (math.pi * math.sqrt(total * LANES))
    smem = pl.BlockSpec(memory_space=pltpu.SMEM)
    vmem = pl.BlockSpec(memory_space=pltpu.VMEM)
    params = pltpu.CompilerParams(vmem_limit_bytes=48 << 20)
    shape = jax.ShapeDtypeStruct
    rows = 3 * count // LANES

    part, outgoing, near, sums = pl.pallas_call(
        functools.partial(prep_kernel, cap),
        out_shape=(
            shape((devices, rows, LANES), F32),
            shape((3, held, LANES), F32),
            shape((DEPTH, points), BF16),
            shape((FEATS, points), BF16),
        ),
        in_specs=[smem, vmem, vmem, vmem],
        out_specs=[vmem] * 4,
        scratch_shapes=[
            pltpu.VMEM((blocks * DEPTH, LANES), F32),
            pltpu.VMEM((blocks * FEATS, LANES), F32),
        ],
        compiler_params=params,
        name="prep",
    )(me, positions, block_links, panel_points)
    parts = lax.all_to_all(part, AXES, split_axis=0, concat_axis=0, tiled=True)
    arrived = lax.all_to_all(outgoing, AXES, split_axis=1, concat_axis=1, tiled=True)
    acc, side, targets = pl.pallas_call(
        functools.partial(pair_kernel, min(points, 2048), 4),
        out_shape=(
            shape((FEATS, count), F32),
            shape((DEPTH, count), BF16),
            shape((3, count), F32),
        ),
        in_specs=[vmem] * 3,
        out_specs=[vmem] * 3,
        scratch_shapes=[pltpu.VMEM((DEPTH, count), F32)],
        compiler_params=params,
        name="pairs",
    )(parts, near, sums)
    smoothed, velocity = pl.pallas_call(
        functools.partial(owner_kernel, cap, scale),
        out_shape=(shape((3, held, LANES), F32), shape((3, count), F32)),
        in_specs=[smem] + [vmem] * 5,
        out_specs=[vmem] * 2,
        scratch_shapes=[
            pltpu.VMEM((devices, LANES), jnp.int32),
            pltpu.VMEM((devices, LANES), jnp.int32),
            pltpu.VMEM((DEPTH, EDGES * held), F32),
            pltpu.VMEM((FEATS, EDGES * held), F32),
        ],
        compiler_params=params,
        name="owners",
    )(me, block_links, arrived, side, targets, acc)
    shares = lax.all_to_all(
        velocity.reshape(3, devices, share), AXES, split_axis=1, concat_axis=1, tiled=True
    )
    return (smoothed, jnp.sum(shares, axis=1)[None])


def solution(mesh):
    placed = (P(None, AXES, None), P(), P())
    return jax.shard_map(
        shards,
        mesh=mesh,
        in_specs=placed,
        out_specs=(P(None, AXES, None), P("row", None, "col")),
        check_vma=False,
    )
```

```python
import functools
import math

import jax
import jax.numpy as jnp
from jax import lax
from jax.experimental import pallas as pl
from jax.experimental.pallas import tpu as pltpu
from jax.sharding import PartitionSpec as P

CORE_SQUARED = 0.01
F32 = jnp.float32
BF16 = jnp.bfloat16
LANES = 128
LANE_BITS = 7
DEPTH = 32
FEATS = 16
EDGES = 5
AXES = ("row", "col")


def iota(shape, dim):
    return lax.broadcasted_iota(jnp.int32, shape, dim)


def three_parts(value):
    first = value.astype(BF16)
    rest = value - first.astype(F32)
    second = rest.astype(BF16)
    third = (rest - second.astype(F32)).astype(BF16)
    return (first, second, third)


def dot(left, right):
    return jnp.dot(left, right, preferred_element_type=F32)


def pick(onehot, value):
    first, second, third = three_parts(value)
    return dot(onehot, first) + dot(onehot, second) + dot(onehot, third)


def as_columns(row):
    return jnp.transpose(jnp.broadcast_to(row.astype(F32), (LANES, row.shape[1])))


def shifted(value, steps):
    return pltpu.roll(value, (-steps) % LANES, 1)


def five_taps(far_left, left, here, right, far_right):
    return (far_left + far_right + 4.0 * (left + right) + 6.0 * here) * 0.0625


def cross(left_vec, right_vec):
    return [
        left_vec[1] * right_vec[2] - left_vec[2] * right_vec[1],
        left_vec[2] * right_vec[0] - left_vec[0] * right_vec[2],
        left_vec[0] * right_vec[1] - left_vec[1] * right_vec[0],
    ]


def source_rows(here, ahead, keep=None):
    segment = [a - h for a, h in zip(ahead, here)]
    centre = [0.5 * (a + h) for a, h in zip(ahead, here)]
    if keep is not None:
        segment = [jnp.where(keep, s, 0.0) for s in segment]
    near = []
    for value in centre:
        one, two, three = [part.astype(F32) for part in three_parts(value)]
        near += [one, two, three, one, two, one]
    norm = centre[0] * centre[0] + centre[1] * centre[1] + centre[2] * centre[2]
    near += [part.astype(F32) for part in three_parts(norm)]
    near += [jnp.ones_like(norm)] * 3
    terms = segment + cross(segment, centre)
    tops = [value.astype(BF16).astype(F32) for value in terms]
    sums = tops + [value - top for value, top in zip(terms, tops)]
    return near, sums


def target_rows(targets):
    rows = []
    for value in targets:
        one, two, three = [part.astype(F32) for part in three_parts(-2.0 * value)]
        rows += [one, one, one, two, two, three]
    norm = targets[0] * targets[0] + targets[1] * targets[1] + targets[2] * targets[2]
    rows += [jnp.ones_like(norm)] * 3
    rows += [part.astype(F32) for part in three_parts(norm + CORE_SQUARED)]
    return rows


def pair_sums(near, sums, target_side):
    squared = lax.dot_general(
        near, target_side, (((0,), (0,)), ((), ())), preferred_element_type=F32
    )
    root = lax.rsqrt(squared)
    weight = root * root * root
    top = weight.astype(BF16)
    rest = (weight - top.astype(F32)).astype(BF16)
    return dot(sums, top) + dot(sums, rest)


def my_place():
    return lax.axis_index("row") * lax.axis_size("col") + lax.axis_index("col")


def fetch(pairs, sems):
    copies = [
        pltpu.make_async_copy(source, target, sems.at[k]) for k, (source, target) in enumerate(pairs)
    ]
    for copy in copies:
        copy.start()
    for copy in copies:
        copy.wait()


def target_kernel(pos_hbm, links_hbm, panel_hbm, keep_ref, send_ref, pos_ref, links_ref, panel_ref, sems):
    fetch([(pos_hbm, pos_ref), (links_hbm, links_ref), (panel_hbm, panel_ref)], sems)
    blocks = pos_ref.shape[1]
    total = links_ref.shape[1]
    base = my_place() * blocks
    mine = pl.ds(pl.multiple_of(base, LANES), blocks)
    lane = iota((blocks, LANES), 1)
    ids = iota((blocks, LANES), 0) + base

    wanted = jnp.concatenate([panel_ref[r : r + 1, :] for r in range(panel_ref.shape[0])], axis=1)
    count = wanted.shape[1]
    wanted_block = lax.shift_right_logical(wanted, LANE_BITS)
    wanted_point = jnp.bitwise_and(wanted, LANES - 1)

    follow_col = as_columns(links_ref[1:2, mine]).astype(jnp.int32)[:, :1]
    found = jnp.zeros((blocks, LANES), F32)
    lane_f = lane.astype(F32)
    for r in range(total // LANES):
        row = links_ref[1:2, r * LANES : (r + 1) * LANES]
        found = found + jnp.where(row == ids, lane_f + float(r * LANES), 0.0)
    precede_col = jnp.sum(found, axis=1, keepdims=True).astype(jnp.int32)

    held_here = wanted_block == (iota((blocks, count), 0) + base)
    before = jnp.logical_and(wanted_point < 2, follow_col == wanted_block)
    after = jnp.logical_and(wanted_point >= LANES - 2, precede_col == wanted_block)
    onehot = jnp.concatenate(
        [
            jnp.where(held_here, 1.0, 0.0).astype(BF16),
            jnp.where(jnp.logical_or(before, after), 1.0, 0.0).astype(BF16),
        ],
        axis=0,
    )

    stacked = []
    for c in range(3):
        x = pos_ref[c]
        rolled = {s: shifted(x, s) for s in (-2, -1, 1, 2)}
        inner = {
            s: jnp.where((lane >= -s) if s < 0 else (lane < LANES - s), v, 0.0)
            for s, v in rolled.items()
        }
        outer = {s: rolled[s] - inner[s] for s in rolled}
        own = five_taps(inner[-2], inner[-1], x, inner[1], inner[2])
        other = five_taps(outer[-2], outer[-1], 0.0, outer[1], outer[2])
        stacked.append(jnp.transpose(jnp.concatenate([own, other], axis=0)))
    one, two, three = three_parts(jnp.concatenate(stacked, axis=0))
    values = dot(one, onehot) + dot(two, onehot) + dot(three, onehot)
    at_point = iota((LANES, count), 0) == wanted_point
    even = lax.rem(lax.axis_index("col"), 2) == 0
    half = count // 2
    per = half // LANES
    for c in range(3):
        part = jnp.where(at_point, values[c * LANES : (c + 1) * LANES], 0.0)
        row = jnp.sum(part, axis=0, keepdims=True)
        for i in range(per):
            low = row[:, i * LANES : (i + 1) * LANES]
            high = row[:, half + i * LANES : half + (i + 1) * LANES]
            at = slice(c * per + i, c * per + i + 1)
            keep_ref[at, :] = jnp.where(even, low, high)
            send_ref[at, :] = jnp.where(even, high, low)


def owner_links(cap, held, me, links_ref, owner_scr, follow_scr):
    devices = owner_scr.shape[0]
    for r in range(devices):
        owner_scr[r : r + 1, :] = links_ref[0:1, r * LANES : (r + 1) * LANES]
        follow_scr[r : r + 1, :] = links_ref[1:2, r * LANES : (r + 1) * LANES]
    owned = jnp.where(owner_scr[...] == me, 1.0, 0.0)
    upper = jnp.where(iota((LANES, LANES), 0) < iota((LANES, LANES), 1), 1.0, 0.0)
    rank = dot(owned.astype(BF16), upper.astype(BF16))
    follow = follow_scr[...]
    table = jnp.concatenate(
        [
            owned,
            rank,
            lax.shift_right_logical(follow, LANE_BITS).astype(F32),
            jnp.bitwise_and(follow, LANES - 1).astype(F32),
        ],
        axis=1,
    ).astype(BF16)
    cap_shift = cap.bit_length() - 1
    slot = iota((held, devices), 0)
    spread = jnp.where(
        lax.shift_right_logical(slot, cap_shift) == iota((held, devices), 1), 1.0, 0.0
    ).astype(BF16)
    wide = dot(spread, table)
    slots = iota((held, LANES), 0)
    seat = jnp.bitwise_and(slots, cap - 1).astype(F32)
    hit = jnp.logical_and(wide[:, :LANES] == 1.0, wide[:, LANES : 2 * LANES] == seat)
    number = (lax.shift_right_logical(slots, cap_shift) * LANES + iota((held, LANES), 1)).astype(F32)
    target_no = wide[:, 2 * LANES : 3 * LANES] * float(LANES) + wide[:, 3 * LANES :]
    live = jnp.sum(jnp.where(hit, 1.0, 0.0), axis=1, keepdims=True)
    id_col = jnp.sum(jnp.where(hit, number, 0.0), axis=1, keepdims=True) + live - 1.0
    next_col = jnp.sum(jnp.where(hit, target_no, 0.0), axis=1, keepdims=True) + 2.0 * live - 2.0
    id_row = jnp.transpose(jnp.broadcast_to(id_col, (held, LANES)))[:1, :]
    next_row = jnp.transpose(jnp.broadcast_to(next_col, (held, LANES)))[:1, :]
    to_next = jnp.where(next_col == id_row, 1.0, 0.0).astype(BF16)
    to_prev = jnp.where(id_col == next_row, 1.0, 0.0).astype(BF16)
    return to_next, to_prev


def source_kernel(cap, pos_ref, links_ref, out_ref, near_ref, sums_ref, next_ref, prev_ref, near_scr, sums_scr, owner_scr, follow_scr):
    me = my_place()
    blocks = pos_ref.shape[1]
    devices = out_ref.shape[0]
    held = devices * cap
    mine = pl.ds(pl.multiple_of(me * blocks, LANES), blocks)
    lane = iota((blocks, LANES), 1)

    owner_row = links_ref[0:1, mine]
    owner_col = as_columns(owner_row).astype(jnp.int32)
    same = jnp.logical_and(owner_col == owner_row, iota((blocks, blocks), 0) < iota((blocks, blocks), 1))
    rank = jnp.sum(jnp.where(same, 1.0, 0.0), axis=0, keepdims=True).astype(jnp.int32)
    slot = owner_row * cap + rank
    into = jnp.where(iota((held, blocks), 0) == slot, 1.0, 0.0).astype(BF16)
    here_all = []
    for c in range(3):
        x = pos_ref[c]
        placed = pick(into, x)
        for d in range(devices):
            out_ref[d, c * cap : (c + 1) * cap, :] = placed[d * cap : (d + 1) * cap, :]
        here_all.append(five_taps(shifted(x, -2), shifted(x, -1), x, shifted(x, 1), shifted(x, 2)))

    ahead_all = [shifted(v, 1) for v in here_all]
    keep = jnp.logical_and(lane >= 2, lane <= LANES - 4)
    near, sums = source_rows(here_all, ahead_all, keep)
    near_scr[...] = jnp.zeros_like(near_scr)
    sums_scr[...] = jnp.zeros_like(sums_scr)
    for k, value in enumerate(near):
        near_scr[pl.ds(k, blocks, stride=DEPTH), :] = value
    for k, value in enumerate(sums):
        sums_scr[pl.ds(k, blocks, stride=FEATS), :] = value
    for b in range(blocks):
        near_ref[:, b * LANES : (b + 1) * LANES] = near_scr[b * DEPTH : (b + 1) * DEPTH, :].astype(BF16)
        sums_ref[:, b * LANES : (b + 1) * LANES] = sums_scr[b * FEATS : (b + 1) * FEATS, :].astype(BF16)
    next_ref[...], prev_ref[...] = owner_links(cap, held, me, links_ref, owner_scr, follow_scr)


def pair_kernel(tile, parts, part_ref, near_ref, sums_ref, acc_ref, side_ref, target_ref, rows_scr):
    halves = []
    for h in range(2):
        added = part_ref[h]
        for d in range(h + 2, part_ref.shape[0], 2):
            added = added + part_ref[d]
        halves.append(added)
    per = part_ref.shape[1] // 3
    targets = [
        jnp.concatenate([v[c * per + i : c * per + i + 1, :] for v in halves for i in range(per)], axis=1)
        for c in range(3)
    ]
    rows_scr[...] = jnp.zeros_like(rows_scr)
    for c in range(3):
        target_ref[c : c + 1, :] = targets[c]
    for k, row in enumerate(target_rows(targets)):
        rows_scr[k : k + 1, :] = row
    side_ref[...] = rows_scr[...].astype(BF16)
    count = side_ref.shape[1]
    piece = tile // parts

    def one_tile(turn, running):
        result = []
        for s in range(parts):
            at = pl.ds(pl.multiple_of(turn * tile + s * piece, piece), piece)
            result.append(running[s] + pair_sums(near_ref[:, at], sums_ref[:, at], side_ref[...]))
        return tuple(result)

    zeros = tuple(jnp.zeros((FEATS, count), F32) for s in range(parts))
    running = lax.fori_loop(0, near_ref.shape[1] // tile, one_tile, zeros)
    acc_ref[...] = sum(running[1:], running[0])


def held_blocks(cap, arrived_ref, x_scr):
    for c in range(3):
        for d in range(arrived_ref.shape[0]):
            x_scr[c, d * cap : (d + 1) * cap, :] = arrived_ref[d, c * cap : (c + 1) * cap, :]


def pick_rows(rows, onehot):
    filled = jnp.concatenate([rows, jnp.zeros((16 - rows.shape[0], rows.shape[1]), F32)], axis=0)
    parts = dot(jnp.concatenate(three_parts(filled), axis=0), onehot)
    return parts[:16] + parts[16:32] + parts[32:]


def taps_down(rows):
    n = rows.shape[0] - 4
    return five_taps(*[rows[k : k + n] for k in range(5)])


def end_kernel(cap, scale, arrived_ref, next_ref, prev_ref, side_ref, target_ref, acc_ref, vel_ref, x_scr, near_scr, sums_scr):
    held_blocks(cap, arrived_ref, x_scr)
    held = x_scr.shape[1]
    turned = [jnp.transpose(x_scr[c]) for c in range(3)]
    after = pick_rows(jnp.concatenate([t[:3] for t in turned], axis=0), prev_ref[...])
    before = pick_rows(jnp.concatenate([t[LANES - 2 :] for t in turned], axis=0), next_ref[...])
    here = []
    ahead = []
    for c in range(3):
        first = taps_down(jnp.concatenate([before[2 * c : 2 * c + 2], turned[c][:5]], axis=0))
        last = taps_down(jnp.concatenate([turned[c][LANES - 5 :], after[3 * c : 3 * c + 3]], axis=0))
        here.append(jnp.concatenate([first[:2], last[:3]], axis=0))
        ahead.append(jnp.concatenate([first[1:], last[1:]], axis=0))
    near, sums = source_rows(here, ahead)
    near_scr[...] = jnp.zeros_like(near_scr)
    sums_scr[...] = jnp.zeros_like(sums_scr)
    for k, value in enumerate(near):
        for e in range(EDGES):
            near_scr[k : k + 1, e * held : (e + 1) * held] = value[e : e + 1, :]
    for k, value in enumerate(sums):
        for e in range(EDGES):
            sums_scr[k : k + 1, e * held : (e + 1) * held] = value[e : e + 1, :]
    acc = acc_ref[...] + pair_sums(near_scr[...].astype(BF16), sums_scr[...].astype(BF16), side_ref[...])
    terms = acc[0:6] + acc[6:12]
    targets = [target_ref[c : c + 1, :] for c in range(3)]
    turned = cross([terms[c : c + 1, :] for c in range(3)], targets)
    for c in range(3):
        vel_ref[c : c + 1, :] = scale * (turned[c] - terms[3 + c : 4 + c, :])


def smooth_kernel(cap, arrived_ref, next_ref, prev_ref, smooth_ref, x_scr):
    held_blocks(cap, arrived_ref, x_scr)
    held = x_scr.shape[1]
    lane = iota((held, LANES), 1)
    blocks = jnp.concatenate([x_scr[c] for c in range(3)], axis=1)
    around = pick(jnp.concatenate([next_ref[...], prev_ref[...]], axis=0), blocks)
    for c in range(3):
        x = x_scr[c]
        after = around[:held, c * LANES : (c + 1) * LANES]
        before = around[held:, c * LANES : (c + 1) * LANES]
        at = [jnp.where(lane < s, shifted(before, -s), shifted(x, -s)) for s in (2, 1)]
        at.append(x)
        at += [jnp.where(lane >= LANES - s, shifted(after, s), shifted(x, s)) for s in (1, 2)]
        smooth_ref[c] = five_taps(*at)


def shards(positions, block_links, panel_points):
    devices = lax.axis_size(AXES)
    blocks = positions.shape[1]
    cap = 2 * blocks // devices
    held = devices * cap
    total = block_links.shape[1]
    points = blocks * LANES
    panel = panel_points.shape[1]
    count = panel_points.shape[0] * panel
    share = panel // lax.axis_size("col")
    scale = 1.0 / (math.pi * math.sqrt(total * LANES))
    vmem = pl.BlockSpec(memory_space=pltpu.VMEM)
    params = pltpu.CompilerParams(vmem_limit_bytes=40 << 20)
    shape = jax.ShapeDtypeStruct
    rows = 3 * count // LANES

    anywhere = pl.BlockSpec(memory_space=pltpu.HBM)
    keep, send = pl.pallas_call(
        target_kernel,
        out_shape=(shape((rows // 2, LANES), F32), shape((rows // 2, LANES), F32)),
        in_specs=[anywhere] * 3,
        out_specs=[vmem] * 2,
        scratch_shapes=[
            pltpu.VMEM(positions.shape, F32),
            pltpu.VMEM(block_links.shape, jnp.int32),
            pltpu.VMEM(panel_points.shape, jnp.int32),
            pltpu.SemaphoreType.DMA((3,)),
        ],
        compiler_params=pltpu.CompilerParams(vmem_limit_bytes=32 << 20),
        name="targets",
    )(*[pltpu.with_memory_space_constraint(v, pltpu.HBM) for v in (positions, block_links, panel_points)])
    other = [(k, k ^ 1) for k in range(lax.axis_size("col"))]
    chip_part = keep + lax.ppermute(send, "col", other)
    part = jnp.broadcast_to(chip_part[None], (devices, rows // 2, LANES))
    parts = lax.all_to_all(part, AXES, split_axis=0, concat_axis=0, tiled=True)
    outgoing, near, sums, to_next, to_prev = pl.pallas_call(
        functools.partial(source_kernel, cap),
        out_shape=(
            shape((devices, 3 * cap, LANES), F32),
            shape((DEPTH, points), BF16),
            shape((FEATS, points), BF16),
            shape((held, held), BF16),
            shape((held, held), BF16),
        ),
        in_specs=[vmem] * 2,
        out_specs=[vmem] * 5,
        scratch_shapes=[
            pltpu.VMEM((blocks * DEPTH, LANES), F32),
            pltpu.VMEM((blocks * FEATS, LANES), F32),
            pltpu.VMEM((devices, LANES), jnp.int32),
            pltpu.VMEM((devices, LANES), jnp.int32),
        ],
        compiler_params=params,
        cost_estimate=pl.CostEstimate(flops=10**9, bytes_accessed=10**7, transcendentals=0),
        name="sources",
    )(positions, block_links)

    arrived = lax.all_to_all(outgoing, AXES, split_axis=0, concat_axis=0, tiled=True)
    acc, side, targets = pl.pallas_call(
        functools.partial(pair_kernel, min(points, 4096), 8),
        out_shape=(
            shape((FEATS, count), F32),
            shape((DEPTH, count), BF16),
            shape((3, count), F32),
        ),
        in_specs=[vmem] * 3,
        out_specs=[vmem] * 3,
        scratch_shapes=[pltpu.VMEM((DEPTH, count), F32)],
        compiler_params=params,
        cost_estimate=pl.CostEstimate(
            flops=2 * points * count * 40, bytes_accessed=10**7, transcendentals=points * count
        ),
        name="pairs",
    )(parts, near, sums)
    velocity = pl.pallas_call(
        functools.partial(end_kernel, cap, scale),
        out_shape=shape((3, count), F32),
        in_specs=[vmem] * 6,
        out_specs=vmem,
        scratch_shapes=[
            pltpu.VMEM((3, held, LANES), F32),
            pltpu.VMEM((DEPTH, EDGES * held), F32),
            pltpu.VMEM((FEATS, EDGES * held), F32),
        ],
        compiler_params=params,
        name="ends",
    )(arrived, to_next, to_prev, side, targets, acc)
    smoothed = pl.pallas_call(
        functools.partial(smooth_kernel, cap),
        out_shape=shape((3, held, LANES), F32),
        in_specs=[vmem] * 3,
        out_specs=vmem,
        scratch_shapes=[pltpu.VMEM((3, held, LANES), F32)],
        compiler_params=params,
        cost_estimate=pl.CostEstimate(flops=10**9, bytes_accessed=10**7, transcendentals=0),
        name="smooth",
    )(arrived, to_next, to_prev)
    shares = lax.all_to_all(
        velocity.reshape(3, devices, share), AXES, split_axis=1, concat_axis=1, tiled=True
    )
    return (smoothed, jnp.sum(shares, axis=1)[None])


def solution(mesh):
    placed = (P(None, AXES, None), P(), P())
    return jax.shard_map(
        shards,
        mesh=mesh,
        in_specs=placed,
        out_specs=(P(None, AXES, None), P("row", None, "col")),
        check_vma=False,
    )
```

```python
import functools
import math

import jax
import jax.numpy as jnp
from jax import lax
from jax.experimental import pallas as pl
from jax.experimental.pallas import tpu as pltpu
from jax.sharding import PartitionSpec as P

CORE_SQUARED = 0.01
F32 = jnp.float32
BF16 = jnp.bfloat16
LANES = 128
LANE_BITS = 7
DEPTH = 32
FEATS = 16
EDGES = 5
AXES = ("row", "col")


def iota(shape, dim):
    return lax.broadcasted_iota(jnp.int32, shape, dim)


def three_parts(value):
    first = value.astype(BF16)
    rest = value - first.astype(F32)
    second = rest.astype(BF16)
    third = (rest - second.astype(F32)).astype(BF16)
    return (first, second, third)


def dot(left, right):
    return jnp.dot(left, right, preferred_element_type=F32)


def pick(onehot, value):
    first, second, third = three_parts(value)
    return dot(onehot, first) + dot(onehot, second) + dot(onehot, third)


def as_columns(row):
    return jnp.transpose(jnp.broadcast_to(row.astype(F32), (LANES, row.shape[1])))


def shifted(value, steps):
    return pltpu.roll(value, (-steps) % LANES, 1)


def five_taps(far_left, left, here, right, far_right):
    return (far_left + far_right + 4.0 * (left + right) + 6.0 * here) * 0.0625


def cross(left_vec, right_vec):
    return [
        left_vec[1] * right_vec[2] - left_vec[2] * right_vec[1],
        left_vec[2] * right_vec[0] - left_vec[0] * right_vec[2],
        left_vec[0] * right_vec[1] - left_vec[1] * right_vec[0],
    ]


def source_rows(here, ahead, keep=None):
    segment = [a - h for a, h in zip(ahead, here)]
    centre = [0.5 * (a + h) for a, h in zip(ahead, here)]
    if keep is not None:
        segment = [jnp.where(keep, s, 0.0) for s in segment]
    near = []
    for value in centre:
        one, two, three = [part.astype(F32) for part in three_parts(value)]
        near += [one, two, three, one, two, one]
    norm = centre[0] * centre[0] + centre[1] * centre[1] + centre[2] * centre[2]
    near += [part.astype(F32) for part in three_parts(norm)]
    near += [jnp.ones_like(norm)] * 3
    terms = segment + cross(segment, centre)
    tops = [value.astype(BF16).astype(F32) for value in terms]
    sums = tops + [value - top for value, top in zip(terms, tops)]
    return near, sums


def target_rows(targets):
    rows = []
    for value in targets:
        one, two, three = [part.astype(F32) for part in three_parts(-2.0 * value)]
        rows += [one, one, one, two, two, three]
    norm = targets[0] * targets[0] + targets[1] * targets[1] + targets[2] * targets[2]
    rows += [jnp.ones_like(norm)] * 3
    rows += [part.astype(F32) for part in three_parts(norm + CORE_SQUARED)]
    return rows


def pair_sums(start, near, sums, target_side):
    squared = lax.dot_general(
        near, target_side, (((0,), (0,)), ((), ())), preferred_element_type=F32
    )
    root = lax.rsqrt(squared)
    weight = root * root * root
    top = weight.astype(BF16)
    rest = (weight - top.astype(F32)).astype(BF16)
    return start + dot(sums, top) + dot(sums, rest)


def my_place():
    return lax.axis_index("row") * lax.axis_size("col") + lax.axis_index("col")


def fetch(pairs, sems):
    copies = [
        pltpu.make_async_copy(source, target, sems.at[k]) for k, (source, target) in enumerate(pairs)
    ]
    for copy in copies:
        copy.start()
    for copy in copies:
        copy.wait()


def target_kernel(pos_hbm, links_hbm, panel_hbm, part_ref, pos_ref, links_ref, panel_ref, sems):
    fetch([(pos_hbm, pos_ref), (links_hbm, links_ref), (panel_hbm, panel_ref)], sems)
    blocks = pos_ref.shape[1]
    total = links_ref.shape[1]
    base = my_place() * blocks
    mine = pl.ds(pl.multiple_of(base, LANES), blocks)
    lane = iota((blocks, LANES), 1)
    ids = iota((blocks, LANES), 0) + base

    wanted = jnp.concatenate([panel_ref[r : r + 1, :] for r in range(panel_ref.shape[0])], axis=1)
    count = wanted.shape[1]
    wanted_block = lax.shift_right_logical(wanted, LANE_BITS)
    wanted_point = jnp.bitwise_and(wanted, LANES - 1)

    follow_col = as_columns(links_ref[1:2, mine]).astype(jnp.int32)[:, :1]
    found = jnp.zeros((blocks, LANES), F32)
    lane_f = lane.astype(F32)
    for r in range(total // LANES):
        row = links_ref[1:2, r * LANES : (r + 1) * LANES]
        found = found + jnp.where(row == ids, lane_f + float(r * LANES), 0.0)
    precede_col = jnp.sum(found, axis=1, keepdims=True).astype(jnp.int32)

    held_here = wanted_block == (iota((blocks, count), 0) + base)
    before = jnp.logical_and(wanted_point < 2, follow_col == wanted_block)
    after = jnp.logical_and(wanted_point >= LANES - 2, precede_col == wanted_block)
    onehot = jnp.concatenate(
        [
            jnp.where(held_here, 1.0, 0.0).astype(BF16),
            jnp.where(jnp.logical_or(before, after), 1.0, 0.0).astype(BF16),
        ],
        axis=0,
    )

    stacked = []
    for c in range(3):
        x = pos_ref[c]
        rolled = {s: shifted(x, s) for s in (-2, -1, 1, 2)}
        inner = {
            s: jnp.where((lane >= -s) if s < 0 else (lane < LANES - s), v, 0.0)
            for s, v in rolled.items()
        }
        outer = {s: rolled[s] - inner[s] for s in rolled}
        own = five_taps(inner[-2], inner[-1], x, inner[1], inner[2])
        other = five_taps(outer[-2], outer[-1], 0.0, outer[1], outer[2])
        stacked.append(jnp.transpose(jnp.concatenate([own, other], axis=0)))
    one, two, three = three_parts(jnp.concatenate(stacked, axis=0))
    values = dot(one, onehot) + dot(two, onehot) + dot(three, onehot)
    at_point = iota((LANES, count), 0) == wanted_point
    per = count // LANES
    for c in range(3):
        part = jnp.where(at_point, values[c * LANES : (c + 1) * LANES], 0.0)
        row = jnp.sum(part, axis=0, keepdims=True)
        for i in range(per):
            part_ref[c * per + i : c * per + i + 1, :] = row[:, i * LANES : (i + 1) * LANES]


def owner_links(cap, held, me, links_ref, owner_scr, follow_scr):
    devices = owner_scr.shape[0]
    for r in range(devices):
        owner_scr[r : r + 1, :] = links_ref[0:1, r * LANES : (r + 1) * LANES]
        follow_scr[r : r + 1, :] = links_ref[1:2, r * LANES : (r + 1) * LANES]
    owned = jnp.where(owner_scr[...] == me, 1.0, 0.0)
    upper = jnp.where(iota((LANES, LANES), 0) < iota((LANES, LANES), 1), 1.0, 0.0)
    rank = dot(owned.astype(BF16), upper.astype(BF16))
    follow = follow_scr[...]
    table = jnp.concatenate(
        [
            owned,
            rank,
            lax.shift_right_logical(follow, LANE_BITS).astype(F32),
            jnp.bitwise_and(follow, LANES - 1).astype(F32),
        ],
        axis=1,
    ).astype(BF16)
    cap_shift = cap.bit_length() - 1
    slot = iota((held, devices), 0)
    spread = jnp.where(
        lax.shift_right_logical(slot, cap_shift) == iota((held, devices), 1), 1.0, 0.0
    ).astype(BF16)
    wide = dot(spread, table)
    slots = iota((held, LANES), 0)
    seat = jnp.bitwise_and(slots, cap - 1).astype(F32)
    hit = jnp.logical_and(wide[:, :LANES] == 1.0, wide[:, LANES : 2 * LANES] == seat)
    number = (lax.shift_right_logical(slots, cap_shift) * LANES + iota((held, LANES), 1)).astype(F32)
    target_no = wide[:, 2 * LANES : 3 * LANES] * float(LANES) + wide[:, 3 * LANES :]
    live = jnp.sum(jnp.where(hit, 1.0, 0.0), axis=1, keepdims=True)
    id_col = jnp.sum(jnp.where(hit, number, 0.0), axis=1, keepdims=True) + live - 1.0
    next_col = jnp.sum(jnp.where(hit, target_no, 0.0), axis=1, keepdims=True) + 2.0 * live - 2.0
    id_row = jnp.transpose(jnp.broadcast_to(id_col, (held, LANES)))[:1, :]
    next_row = jnp.transpose(jnp.broadcast_to(next_col, (held, LANES)))[:1, :]
    to_next = jnp.where(next_col == id_row, 1.0, 0.0).astype(BF16)
    to_prev = jnp.where(id_col == next_row, 1.0, 0.0).astype(BF16)
    return to_next, to_prev


def source_kernel(cap, pos_ref, links_ref, out_ref, near_ref, sums_ref, next_ref, prev_ref, near_scr, sums_scr, owner_scr, follow_scr):
    me = my_place()
    blocks = pos_ref.shape[1]
    devices = out_ref.shape[0]
    held = devices * cap
    mine = pl.ds(pl.multiple_of(me * blocks, LANES), blocks)
    lane = iota((blocks, LANES), 1)

    owner_row = links_ref[0:1, mine]
    owner_col = as_columns(owner_row).astype(jnp.int32)
    same = jnp.logical_and(owner_col == owner_row, iota((blocks, blocks), 0) < iota((blocks, blocks), 1))
    rank = jnp.sum(jnp.where(same, 1.0, 0.0), axis=0, keepdims=True).astype(jnp.int32)
    slot = owner_row * cap + rank
    into = jnp.where(iota((held, blocks), 0) == slot, 1.0, 0.0).astype(BF16)
    here_all = []
    for c in range(3):
        x = pos_ref[c]
        placed = pick(into, x)
        for d in range(devices):
            out_ref[d, c * cap : (c + 1) * cap, :] = placed[d * cap : (d + 1) * cap, :]
        here_all.append(five_taps(shifted(x, -2), shifted(x, -1), x, shifted(x, 1), shifted(x, 2)))

    ahead_all = [shifted(v, 1) for v in here_all]
    keep = jnp.logical_and(lane >= 2, lane <= LANES - 4)
    near, sums = source_rows(here_all, ahead_all, keep)
    near_scr[...] = jnp.zeros_like(near_scr)
    sums_scr[...] = jnp.zeros_like(sums_scr)
    for k, value in enumerate(near):
        near_scr[pl.ds(k, blocks, stride=DEPTH), :] = value
    for k, value in enumerate(sums):
        sums_scr[pl.ds(k, blocks, stride=FEATS), :] = value
    for b in range(blocks):
        near_ref[:, b * LANES : (b + 1) * LANES] = near_scr[b * DEPTH : (b + 1) * DEPTH, :].astype(BF16)
        sums_ref[:, b * LANES : (b + 1) * LANES] = sums_scr[b * FEATS : (b + 1) * FEATS, :].astype(BF16)
    next_ref[...], prev_ref[...] = owner_links(cap, held, me, links_ref, owner_scr, follow_scr)


def pair_kernel(tile, parts, part_ref, near_ref, sums_ref, acc_ref, side_ref, target_ref, rows_scr):
    per = part_ref.shape[0] // 3
    targets = [
        jnp.concatenate([part_ref[c * per + i : c * per + i + 1, :] for i in range(per)], axis=1)
        for c in range(3)
    ]
    rows_scr[...] = jnp.zeros_like(rows_scr)
    for c in range(3):
        target_ref[c : c + 1, :] = targets[c]
    for k, row in enumerate(target_rows(targets)):
        rows_scr[k : k + 1, :] = row
    side_ref[...] = rows_scr[...].astype(BF16)
    count = side_ref.shape[1]
    piece = tile // parts

    def one_tile(turn, running):
        for s in range(parts):
            at = pl.ds(pl.multiple_of(turn * tile + s * piece, piece), piece)
            running = pair_sums(running, near_ref[:, at], sums_ref[:, at], side_ref[...])
        return running

    acc_ref[...] = lax.fori_loop(
        0, near_ref.shape[1] // tile, one_tile, jnp.zeros((FEATS, count), F32)
    )


def held_blocks(cap, arrived_ref, x_scr):
    for c in range(3):
        for d in range(arrived_ref.shape[0]):
            x_scr[c, d * cap : (d + 1) * cap, :] = arrived_ref[d, c * cap : (c + 1) * cap, :]


def pick_rows(rows, onehot):
    filled = jnp.concatenate([rows, jnp.zeros((16 - rows.shape[0], rows.shape[1]), F32)], axis=0)
    parts = dot(jnp.concatenate(three_parts(filled), axis=0), onehot)
    return parts[:16] + parts[16:32] + parts[32:]


def taps_down(rows):
    n = rows.shape[0] - 4
    return five_taps(*[rows[k : k + n] for k in range(5)])


def end_kernel(cap, scale, arrived_ref, next_ref, prev_ref, side_ref, target_ref, acc_ref, vel_ref, x_scr, near_scr, sums_scr):
    held_blocks(cap, arrived_ref, x_scr)
    held = x_scr.shape[1]
    turned = [jnp.transpose(x_scr[c]) for c in range(3)]
    after = pick_rows(jnp.concatenate([t[:3] for t in turned], axis=0), prev_ref[...])
    before = pick_rows(jnp.concatenate([t[LANES - 2 :] for t in turned], axis=0), next_ref[...])
    here = []
    ahead = []
    for c in range(3):
        first = taps_down(jnp.concatenate([before[2 * c : 2 * c + 2], turned[c][:5]], axis=0))
        last = taps_down(jnp.concatenate([turned[c][LANES - 5 :], after[3 * c : 3 * c + 3]], axis=0))
        here.append(jnp.concatenate([first[:2], last[:3]], axis=0))
        ahead.append(jnp.concatenate([first[1:], last[1:]], axis=0))
    near, sums = source_rows(here, ahead)
    near_scr[...] = jnp.zeros_like(near_scr)
    sums_scr[...] = jnp.zeros_like(sums_scr)
    for k, value in enumerate(near):
        for e in range(EDGES):
            near_scr[k : k + 1, e * held : (e + 1) * held] = value[e : e + 1, :]
    for k, value in enumerate(sums):
        for e in range(EDGES):
            sums_scr[k : k + 1, e * held : (e + 1) * held] = value[e : e + 1, :]
    acc = pair_sums(acc_ref[...], near_scr[...].astype(BF16), sums_scr[...].astype(BF16), side_ref[...])
    terms = acc[0:6] + acc[6:12]
    targets = [target_ref[c : c + 1, :] for c in range(3)]
    turned = cross([terms[c : c + 1, :] for c in range(3)], targets)
    velocity = jnp.concatenate(
        [scale * (turned[c] - terms[3 + c : 4 + c, :]) for c in range(3)], axis=0
    )
    share = vel_ref.shape[2]
    for d in range(vel_ref.shape[0]):
        vel_ref[d] = velocity[:, d * share : (d + 1) * share]


def smooth_kernel(cap, arrived_ref, next_ref, prev_ref, smooth_ref, x_scr):
    held_blocks(cap, arrived_ref, x_scr)
    held = x_scr.shape[1]
    lane = iota((held, LANES), 1)
    blocks = jnp.concatenate([x_scr[c] for c in range(3)], axis=1)
    around = pick(jnp.concatenate([next_ref[...], prev_ref[...]], axis=0), blocks)
    for c in range(3):
        x = x_scr[c]
        after = around[:held, c * LANES : (c + 1) * LANES]
        before = around[held:, c * LANES : (c + 1) * LANES]
        at = [jnp.where(lane < s, shifted(before, -s), shifted(x, -s)) for s in (2, 1)]
        at.append(x)
        at += [jnp.where(lane >= LANES - s, shifted(after, s), shifted(x, s)) for s in (1, 2)]
        smooth_ref[c] = five_taps(*at)


def swapped(value, axis, steps):
    size = lax.axis_size(axis)
    return [lax.ppermute(value, axis, [(k, k ^ step) for k in range(size)]) for step in steps]


def shards(positions, block_links, panel_points):
    devices = lax.axis_size(AXES)
    blocks = positions.shape[1]
    cap = 2 * blocks // devices
    held = devices * cap
    total = block_links.shape[1]
    points = blocks * LANES
    panel = panel_points.shape[1]
    count = panel_points.shape[0] * panel
    share = panel // lax.axis_size("col")
    scale = 1.0 / (math.pi * math.sqrt(total * LANES))
    vmem = pl.BlockSpec(memory_space=pltpu.VMEM)
    params = pltpu.CompilerParams(vmem_limit_bytes=40 << 20)
    shape = jax.ShapeDtypeStruct
    rows = 3 * count // LANES

    anywhere = pl.BlockSpec(memory_space=pltpu.HBM)
    part = pl.pallas_call(
        target_kernel,
        out_shape=shape((rows, LANES), F32),
        in_specs=[anywhere] * 3,
        out_specs=vmem,
        scratch_shapes=[
            pltpu.VMEM(positions.shape, F32),
            pltpu.VMEM(block_links.shape, jnp.int32),
            pltpu.VMEM(panel_points.shape, jnp.int32),
            pltpu.SemaphoreType.DMA((3,)),
        ],
        compiler_params=pltpu.CompilerParams(vmem_limit_bytes=32 << 20),
        name="targets",
    )(*[pltpu.with_memory_space_constraint(v, pltpu.HBM) for v in (positions, block_links, panel_points)])
    part = part + swapped(part, "col", [1])[0]
    part, positions = lax.optimization_barrier((part, positions))
    part = sum(swapped(part, "row", range(1, lax.axis_size("row"))), part)
    outgoing, near, sums, to_next, to_prev = pl.pallas_call(
        functools.partial(source_kernel, cap),
        out_shape=(
            shape((devices, 3 * cap, LANES), F32),
            shape((DEPTH, points), BF16),
            shape((FEATS, points), BF16),
            shape((held, held), BF16),
            shape((held, held), BF16),
        ),
        in_specs=[vmem] * 2,
        out_specs=[vmem] * 5,
        scratch_shapes=[
            pltpu.VMEM((blocks * DEPTH, LANES), F32),
            pltpu.VMEM((blocks * FEATS, LANES), F32),
            pltpu.VMEM((devices, LANES), jnp.int32),
            pltpu.VMEM((devices, LANES), jnp.int32),
        ],
        compiler_params=params,
        cost_estimate=pl.CostEstimate(flops=10**9, bytes_accessed=10**7, transcendentals=0),
        name="sources",
    )(positions, block_links)

    outgoing, part = lax.optimization_barrier((outgoing, part))
    near_by = part + swapped(part, "col", [2])[0]
    parts = near_by + swapped(near_by, "col", [4])[0]
    arrived = lax.all_to_all(outgoing, AXES, split_axis=0, concat_axis=0, tiled=True)
    acc, side, targets = pl.pallas_call(
        functools.partial(pair_kernel, min(points, 8192), 16),
        out_shape=(
            shape((FEATS, count), F32),
            shape((DEPTH, count), BF16),
            shape((3, count), F32),
        ),
        in_specs=[vmem] * 3,
        out_specs=[vmem] * 3,
        scratch_shapes=[pltpu.VMEM((DEPTH, count), F32)],
        compiler_params=params,
        cost_estimate=pl.CostEstimate(
            flops=2 * points * count * 1000, bytes_accessed=10**7, transcendentals=0
        ),
        name="pairs",
    )(parts, near, sums)
    velocity = pl.pallas_call(
        functools.partial(end_kernel, cap, scale),
        out_shape=shape((devices, 3, share), F32),
        in_specs=[vmem] * 6,
        out_specs=vmem,
        scratch_shapes=[
            pltpu.VMEM((3, held, LANES), F32),
            pltpu.VMEM((DEPTH, EDGES * held), F32),
            pltpu.VMEM((FEATS, EDGES * held), F32),
        ],
        compiler_params=params,
        name="ends",
    )(arrived, to_next, to_prev, side, targets, acc)
    smoothed = pl.pallas_call(
        functools.partial(smooth_kernel, cap),
        out_shape=shape((3, held, LANES), F32),
        in_specs=[vmem] * 3,
        out_specs=vmem,
        scratch_shapes=[pltpu.VMEM((3, held, LANES), F32)],
        compiler_params=params,
        cost_estimate=pl.CostEstimate(flops=10**9, bytes_accessed=10**7, transcendentals=0),
        name="smooth",
    )(arrived, to_next, to_prev)
    shares = lax.all_to_all(velocity, AXES, split_axis=0, concat_axis=0, tiled=True)
    return (smoothed, jnp.sum(shares, axis=0)[None])


def solution(mesh):
    placed = (P(None, AXES, None), P(), P())
    return jax.shard_map(
        shards,
        mesh=mesh,
        in_specs=placed,
        out_specs=(P(None, AXES, None), P("row", None, "col")),
        check_vma=False,
    )
```

```python
import functools
import math

import jax
import jax.numpy as jnp
from jax import lax
from jax.experimental import pallas as pl
from jax.experimental.pallas import tpu as pltpu
from jax.sharding import PartitionSpec as P

CORE_SQUARED = 0.01
F32 = jnp.float32
BF16 = jnp.bfloat16
LANES = 128
LANE_BITS = 7
DEPTH = 32
FEATS = 16
EDGES = 5
EPIECE = 2
AXES = ("row", "col")


def iota(shape, dim):
    return lax.broadcasted_iota(jnp.int32, shape, dim)


def three_parts(value):
    first = value.astype(BF16)
    rest = value - first.astype(F32)
    second = rest.astype(BF16)
    third = (rest - second.astype(F32)).astype(BF16)
    return (first, second, third)


def dot(left, right):
    return jnp.dot(left, right, preferred_element_type=F32)


def pick(onehot, value):
    first, second, third = three_parts(value)
    return dot(onehot, first) + dot(onehot, second) + dot(onehot, third)


def as_columns(row):
    return jnp.transpose(jnp.broadcast_to(row.astype(F32), (LANES, row.shape[1])))


def shifted(value, steps):
    return pltpu.roll(value, (-steps) % LANES, 1)


def five_taps(far_left, left, here, right, far_right):
    return (far_left + far_right + 4.0 * (left + right) + 6.0 * here) * 0.0625


def cross(left_vec, right_vec):
    return [
        left_vec[1] * right_vec[2] - left_vec[2] * right_vec[1],
        left_vec[2] * right_vec[0] - left_vec[0] * right_vec[2],
        left_vec[0] * right_vec[1] - left_vec[1] * right_vec[0],
    ]


def source_rows(here, ahead, keep=None):
    segment = [a - h for a, h in zip(ahead, here)]
    centre = [0.5 * (a + h) for a, h in zip(ahead, here)]
    if keep is not None:
        segment = [jnp.where(keep, s, 0.0) for s in segment]
    near = []
    for value in centre:
        one, two, three = [part.astype(F32) for part in three_parts(value)]
        near += [one, two, three, one, two, one]
    norm = centre[0] * centre[0] + centre[1] * centre[1] + centre[2] * centre[2]
    near += [part.astype(F32) for part in three_parts(norm)]
    near += [jnp.ones_like(norm)] * 3
    terms = segment + cross(segment, centre)
    tops = [value.astype(BF16).astype(F32) for value in terms]
    sums = tops + [value - top for value, top in zip(terms, tops)]
    return near, sums


def target_rows(targets):
    rows = []
    for value in targets:
        one, two, three = [part.astype(F32) for part in three_parts(-2.0 * value)]
        rows += [one, one, one, two, two, three]
    norm = targets[0] * targets[0] + targets[1] * targets[1] + targets[2] * targets[2]
    rows += [jnp.ones_like(norm)] * 3
    rows += [part.astype(F32) for part in three_parts(norm + CORE_SQUARED)]
    return rows


def pair_sums(start, near, sums, target_side):
    squared = lax.dot_general(
        near, target_side, (((0,), (0,)), ((), ())), preferred_element_type=F32
    )
    root = lax.rsqrt(squared)
    weight = root * root * root
    top = weight.astype(BF16)
    rest = (weight - top.astype(F32)).astype(BF16)
    return start + dot(sums, top) + dot(sums, rest)


def my_place():
    return lax.axis_index("row") * lax.axis_size("col") + lax.axis_index("col")


def target_kernel(pos_hbm, links_hbm, panel_hbm, part_ref, pos_ref, links_ref, panel_ref, sems):
    links_in = pltpu.make_async_copy(links_hbm, links_ref, sems.at[0])
    panel_in = pltpu.make_async_copy(panel_hbm, panel_ref, sems.at[1])
    pos_in = pltpu.make_async_copy(pos_hbm, pos_ref, sems.at[2])
    links_in.start()
    panel_in.start()
    pos_in.start()
    links_in.wait()
    panel_in.wait()
    blocks = pos_ref.shape[1]
    total = links_ref.shape[1]
    base = my_place() * blocks
    mine = pl.ds(pl.multiple_of(base, LANES), blocks)
    lane = iota((blocks, LANES), 1)
    ids = iota((blocks, LANES), 0) + base

    wanted = jnp.concatenate([panel_ref[r : r + 1, :] for r in range(panel_ref.shape[0])], axis=1)
    count = wanted.shape[1]
    wanted_block = lax.shift_right_logical(wanted, LANE_BITS)
    wanted_point = jnp.bitwise_and(wanted, LANES - 1)

    follow_col = as_columns(links_ref[1:2, mine]).astype(jnp.int32)[:, :1]
    found = jnp.zeros((blocks, LANES), F32)
    lane_f = lane.astype(F32)
    for r in range(total // LANES):
        row = links_ref[1:2, r * LANES : (r + 1) * LANES]
        found = found + jnp.where(row == ids, lane_f + float(r * LANES), 0.0)
    precede_col = jnp.sum(found, axis=1, keepdims=True).astype(jnp.int32)

    held_here = wanted_block == (iota((blocks, count), 0) + base)
    before = jnp.logical_and(wanted_point < 2, follow_col == wanted_block)
    after = jnp.logical_and(wanted_point >= LANES - 2, precede_col == wanted_block)
    onehot = jnp.concatenate(
        [
            jnp.where(held_here, 1.0, 0.0).astype(BF16),
            jnp.where(jnp.logical_or(before, after), 1.0, 0.0).astype(BF16),
        ],
        axis=0,
    )

    pos_in.wait()
    stacked = []
    for c in range(3):
        x = pos_ref[c]
        rolled = {s: shifted(x, s) for s in (-2, -1, 1, 2)}
        inner = {
            s: jnp.where((lane >= -s) if s < 0 else (lane < LANES - s), v, 0.0)
            for s, v in rolled.items()
        }
        outer = {s: rolled[s] - inner[s] for s in rolled}
        own = five_taps(inner[-2], inner[-1], x, inner[1], inner[2])
        other = five_taps(outer[-2], outer[-1], 0.0, outer[1], outer[2])
        stacked.append(jnp.transpose(jnp.concatenate([own, other], axis=0)))
    one, two, three = three_parts(jnp.concatenate(stacked, axis=0))
    values = dot(one, onehot) + dot(two, onehot) + dot(three, onehot)
    at_point = iota((LANES, count), 0) == wanted_point
    per = count // LANES
    for c in range(3):
        part = jnp.where(at_point, values[c * LANES : (c + 1) * LANES], 0.0)
        row = jnp.sum(part, axis=0, keepdims=True)
        for i in range(per):
            part_ref[c * per + i : c * per + i + 1, :] = row[:, i * LANES : (i + 1) * LANES]


def owner_links(cap, held, me, links_ref, owner_scr, follow_scr):
    devices = owner_scr.shape[0]
    for r in range(devices):
        owner_scr[r : r + 1, :] = links_ref[0:1, r * LANES : (r + 1) * LANES]
        follow_scr[r : r + 1, :] = links_ref[1:2, r * LANES : (r + 1) * LANES]
    owned = jnp.where(owner_scr[...] == me, 1.0, 0.0)
    upper = jnp.where(iota((LANES, LANES), 0) < iota((LANES, LANES), 1), 1.0, 0.0)
    rank = dot(owned.astype(BF16), upper.astype(BF16))
    follow = follow_scr[...]
    table = jnp.concatenate(
        [
            owned,
            rank,
            lax.shift_right_logical(follow, LANE_BITS).astype(F32),
            jnp.bitwise_and(follow, LANES - 1).astype(F32),
        ],
        axis=1,
    ).astype(BF16)
    cap_shift = cap.bit_length() - 1
    slot = iota((held, devices), 0)
    spread = jnp.where(
        lax.shift_right_logical(slot, cap_shift) == iota((held, devices), 1), 1.0, 0.0
    ).astype(BF16)
    wide = dot(spread, table)
    slots = iota((held, LANES), 0)
    seat = jnp.bitwise_and(slots, cap - 1).astype(F32)
    hit = jnp.logical_and(wide[:, :LANES] == 1.0, wide[:, LANES : 2 * LANES] == seat)
    number = (lax.shift_right_logical(slots, cap_shift) * LANES + iota((held, LANES), 1)).astype(F32)
    target_no = wide[:, 2 * LANES : 3 * LANES] * float(LANES) + wide[:, 3 * LANES :]
    live = jnp.sum(jnp.where(hit, 1.0, 0.0), axis=1, keepdims=True)
    id_col = jnp.sum(jnp.where(hit, number, 0.0), axis=1, keepdims=True) + live - 1.0
    next_col = jnp.sum(jnp.where(hit, target_no, 0.0), axis=1, keepdims=True) + 2.0 * live - 2.0
    id_row = jnp.transpose(jnp.broadcast_to(id_col, (held, LANES)))[:1, :]
    next_row = jnp.transpose(jnp.broadcast_to(next_col, (held, LANES)))[:1, :]
    to_next = jnp.where(next_col == id_row, 1.0, 0.0).astype(BF16)
    to_prev = jnp.where(id_col == next_row, 1.0, 0.0).astype(BF16)
    return to_next, to_prev


def owner_kernel(cap, pos_ref, links_ref, out_ref):
    blocks = pos_ref.shape[1]
    devices = out_ref.shape[0]
    held = devices * cap
    mine = pl.ds(pl.multiple_of(my_place() * blocks, LANES), blocks)
    owner_row = links_ref[0:1, mine]
    owner_col = as_columns(owner_row).astype(jnp.int32)
    same = jnp.logical_and(owner_col == owner_row, iota((blocks, blocks), 0) < iota((blocks, blocks), 1))
    rank = jnp.sum(jnp.where(same, 1.0, 0.0), axis=0, keepdims=True).astype(jnp.int32)
    slot = owner_row * cap + rank
    into = jnp.where(iota((held, blocks), 0) == slot, 1.0, 0.0).astype(BF16)
    placed = pick(into, jnp.concatenate([pos_ref[c] for c in range(3)], axis=1))
    for c in range(3):
        for d in range(devices):
            out_ref[d, c * cap : (c + 1) * cap, :] = placed[
                d * cap : (d + 1) * cap, c * LANES : (c + 1) * LANES
            ]


def source_kernel(cap, pos_ref, links_ref, near_ref, sums_ref, next_ref, prev_ref, owner_scr, follow_scr):
    blocks = pos_ref.shape[1]
    lane = iota((blocks, LANES), 1)
    here_all = []
    for c in range(3):
        x = pos_ref[c]
        here_all.append(five_taps(shifted(x, -2), shifted(x, -1), x, shifted(x, 1), shifted(x, 2)))
    ahead_all = [shifted(v, 1) for v in here_all]
    keep = jnp.logical_and(lane >= 2, lane <= LANES - 4)
    near, sums = source_rows(here_all, ahead_all, keep)
    near += [jnp.zeros_like(near[0])] * (DEPTH - len(near))
    sums += [jnp.zeros_like(sums[0])] * (FEATS - len(sums))
    for rows, out_ref in ((near, near_ref), (sums, sums_ref)):
        by_block = jnp.transpose(jnp.stack(rows), (1, 0, 2)).astype(BF16)
        for b in range(blocks):
            out_ref[:, b * LANES : (b + 1) * LANES] = by_block[b]
    held = next_ref.shape[0]
    next_ref[...], prev_ref[...] = owner_links(cap, held, my_place(), links_ref, owner_scr, follow_scr)


def pair_kernel(tile, parts, part_ref, near_ref, sums_ref, acc_ref, side_ref, target_ref, rows_scr):
    per = part_ref.shape[0] // 3
    targets = [
        jnp.concatenate([part_ref[c * per + i : c * per + i + 1, :] for i in range(per)], axis=1)
        for c in range(3)
    ]
    rows_scr[...] = jnp.zeros_like(rows_scr)
    for c in range(3):
        target_ref[c : c + 1, :] = targets[c]
    for k, row in enumerate(target_rows(targets)):
        rows_scr[k : k + 1, :] = row
    side_ref[...] = rows_scr[...].astype(BF16)
    count = side_ref.shape[1]
    piece = tile // parts

    def one_tile(turn, running):
        for s in range(parts):
            at = pl.ds(pl.multiple_of(turn * tile + s * piece, piece), piece)
            running = pair_sums(running, near_ref[:, at], sums_ref[:, at], side_ref[...])
        return running

    acc_ref[...] = lax.fori_loop(
        0, near_ref.shape[1] // tile, one_tile, jnp.zeros((FEATS, count), F32)
    )


def held_blocks(cap, arrived_ref, x_scr):
    for c in range(3):
        for d in range(arrived_ref.shape[0]):
            x_scr[c, d * cap : (d + 1) * cap, :] = arrived_ref[d, c * cap : (c + 1) * cap, :]


def pick_rows(rows, onehot):
    filled = jnp.concatenate([rows, jnp.zeros((16 - rows.shape[0], rows.shape[1]), F32)], axis=0)
    parts = dot(jnp.concatenate(three_parts(filled), axis=0), onehot)
    return parts[:16] + parts[16:32] + parts[32:]


def taps_down(rows):
    n = rows.shape[0] - 4
    return five_taps(*[rows[k : k + n] for k in range(5)])


def end_kernel(cap, scale, share, arrived_ref, next_ref, prev_ref, side_ref, target_ref, acc_ref, vel_ref, x_scr, near_scr, sums_scr):
    held_blocks(cap, arrived_ref, x_scr)
    held = x_scr.shape[1]
    turned = [jnp.transpose(x_scr[c]) for c in range(3)]
    after = pick_rows(jnp.concatenate([t[:3] for t in turned], axis=0), prev_ref[...])
    before = pick_rows(jnp.concatenate([t[LANES - 2 :] for t in turned], axis=0), next_ref[...])
    here = []
    ahead = []
    for c in range(3):
        first = taps_down(jnp.concatenate([before[2 * c : 2 * c + 2], turned[c][:5]], axis=0))
        last = taps_down(jnp.concatenate([turned[c][LANES - 5 :], after[3 * c : 3 * c + 3]], axis=0))
        here.append(jnp.concatenate([first[:2], last[:3]], axis=0))
        ahead.append(jnp.concatenate([first[1:], last[1:]], axis=0))
    near, sums = source_rows(here, ahead)
    near_scr[...] = jnp.zeros_like(near_scr)
    sums_scr[...] = jnp.zeros_like(sums_scr)
    for k, value in enumerate(near):
        for e in range(EDGES):
            near_scr[k : k + 1, e * held : (e + 1) * held] = value[e : e + 1, :]
    for k, value in enumerate(sums):
        for e in range(EDGES):
            sums_scr[k : k + 1, e * held : (e + 1) * held] = value[e : e + 1, :]
    acc = acc_ref[...]
    for e in range(0, EDGES * held, EPIECE * held):
        at = slice(e, min(e + EPIECE * held, EDGES * held))
        acc = pair_sums(acc, near_scr[:, at].astype(BF16), sums_scr[:, at].astype(BF16), side_ref[...])
    terms = acc[0:6] + acc[6:12]
    targets = [target_ref[c : c + 1, :] for c in range(3)]
    turned = cross([terms[c : c + 1, :] for c in range(3)], targets)
    velocity = jnp.concatenate(
        [scale * (turned[c] - terms[3 + c : 4 + c, :]) for c in range(3)], axis=0
    )
    group = LANES // share
    for d in range(vel_ref.shape[0]):
        vel_ref[d] = velocity[:, d // group * LANES : (d // group + 1) * LANES]


def smooth_kernel(cap, arrived_ref, next_ref, prev_ref, smooth_ref, x_scr):
    held_blocks(cap, arrived_ref, x_scr)
    held = x_scr.shape[1]
    lane = iota((held, LANES), 1)
    blocks = jnp.concatenate([x_scr[c] for c in range(3)], axis=1)
    around = pick(jnp.concatenate([next_ref[...], prev_ref[...]], axis=0), blocks)
    for c in range(3):
        x = x_scr[c]
        after = around[:held, c * LANES : (c + 1) * LANES]
        before = around[held:, c * LANES : (c + 1) * LANES]
        at = [jnp.where(lane < s, shifted(before, -s), shifted(x, -s)) for s in (2, 1)]
        at.append(x)
        at += [jnp.where(lane >= LANES - s, shifted(after, s), shifted(x, s)) for s in (1, 2)]
        smooth_ref[c] = five_taps(*at)


def swapped(value, axis, steps):
    size = lax.axis_size(axis)
    return [lax.ppermute(value, axis, [(k, k ^ step) for k in range(size)]) for step in steps]


def shards(positions, block_links, panel_points):
    devices = lax.axis_size(AXES)
    blocks = positions.shape[1]
    cap = 2 * blocks // devices
    held = devices * cap
    total = block_links.shape[1]
    points = blocks * LANES
    panel = panel_points.shape[1]
    count = panel_points.shape[0] * panel
    share = panel // lax.axis_size("col")
    scale = 1.0 / (math.pi * math.sqrt(total * LANES))
    vmem = pl.BlockSpec(memory_space=pltpu.VMEM)
    params = pltpu.CompilerParams(vmem_limit_bytes=40 << 20)
    shape = jax.ShapeDtypeStruct
    rows = 3 * count // LANES

    anywhere = pl.BlockSpec(memory_space=pltpu.HBM)
    part = pl.pallas_call(
        target_kernel,
        out_shape=shape((rows, LANES), F32),
        in_specs=[anywhere] * 3,
        out_specs=vmem,
        scratch_shapes=[
            pltpu.VMEM(positions.shape, F32),
            pltpu.VMEM(block_links.shape, jnp.int32),
            pltpu.VMEM(panel_points.shape, jnp.int32),
            pltpu.SemaphoreType.DMA((3,)),
        ],
        compiler_params=pltpu.CompilerParams(vmem_limit_bytes=32 << 20),
        name="targets",
    )(*[pltpu.with_memory_space_constraint(v, pltpu.HBM) for v in (positions, block_links, panel_points)])
    part, positions, block_links = lax.optimization_barrier((part, positions, block_links))
    outgoing = pl.pallas_call(
        functools.partial(owner_kernel, cap),
        out_shape=shape((devices, 3 * cap, LANES), F32),
        in_specs=[vmem] * 2,
        out_specs=vmem,
        compiler_params=params,
        cost_estimate=pl.CostEstimate(flops=10**9, bytes_accessed=10**6, transcendentals=0),
        name="outgoing",
    )(positions, block_links)
    part = part + swapped(part, "col", [1])[0]
    part, positions, outgoing = lax.optimization_barrier((part, positions, outgoing))
    part = sum(swapped(part, "row", range(1, lax.axis_size("row"))), part)
    near, sums, to_next, to_prev = pl.pallas_call(
        functools.partial(source_kernel, cap),
        out_shape=(
            shape((DEPTH, points), BF16),
            shape((FEATS, points), BF16),
            shape((held, held), BF16),
            shape((held, held), BF16),
        ),
        in_specs=[vmem] * 2,
        out_specs=[vmem] * 4,
        scratch_shapes=[
            pltpu.VMEM((devices, LANES), jnp.int32),
            pltpu.VMEM((devices, LANES), jnp.int32),
        ],
        compiler_params=params,
        cost_estimate=pl.CostEstimate(flops=10**9, bytes_accessed=10**7, transcendentals=0),
        name="sources",
    )(positions, block_links)
    near, part = lax.optimization_barrier((near, part))
    outgoing, part = lax.optimization_barrier((outgoing, part))
    far = swapped(part, "col", range(2, lax.axis_size("col"), 2))
    parts = sum(far, part)
    arrived = lax.all_to_all(outgoing, AXES, split_axis=0, concat_axis=0, tiled=True)
    acc, side, targets = pl.pallas_call(
        functools.partial(pair_kernel, min(points, 8192), 16),
        out_shape=(
            shape((FEATS, count), F32),
            shape((DEPTH, count), BF16),
            shape((3, count), F32),
        ),
        in_specs=[vmem] * 3,
        out_specs=[vmem] * 3,
        scratch_shapes=[pltpu.VMEM((DEPTH, count), F32)],
        compiler_params=params,
        cost_estimate=pl.CostEstimate(
            flops=2 * points * count * 1000, bytes_accessed=10**7, transcendentals=0
        ),
        name="pairs",
    )(parts, near, sums)
    velocity = pl.pallas_call(
        functools.partial(end_kernel, cap, scale, share),
        out_shape=shape((devices, 3, LANES), F32),
        in_specs=[vmem] * 6,
        out_specs=vmem,
        scratch_shapes=[
            pltpu.VMEM((3, held, LANES), F32),
            pltpu.VMEM((DEPTH, EDGES * held), F32),
            pltpu.VMEM((FEATS, EDGES * held), F32),
        ],
        compiler_params=params,
        name="ends",
    )(arrived, to_next, to_prev, side, targets, acc)
    smoothed = pl.pallas_call(
        functools.partial(smooth_kernel, cap),
        out_shape=shape((3, held, LANES), F32),
        in_specs=[vmem] * 3,
        out_specs=vmem,
        scratch_shapes=[pltpu.VMEM((3, held, LANES), F32)],
        compiler_params=params,
        cost_estimate=pl.CostEstimate(flops=10**9, bytes_accessed=10**7, transcendentals=0),
        name="smooth",
    )(arrived, to_next, to_prev)
    shares = lax.all_to_all(velocity, AXES, split_axis=0, concat_axis=0, tiled=True)
    start = my_place() % (LANES // share) * share
    summed = lax.dynamic_slice_in_dim(jnp.sum(shares, axis=0), start, share, 1)
    return (smoothed, summed[None])


def solution(mesh):
    placed = (P(None, AXES, None), P(), P())
    return jax.shard_map(
        shards,
        mesh=mesh,
        in_specs=placed,
        out_specs=(P(None, AXES, None), P("row", None, "col")),
        check_vma=False,
    )
```

```python
import functools
import math

import jax
import jax.numpy as jnp
from jax import lax
from jax.experimental import pallas as pl
from jax.experimental.pallas import tpu as pltpu
from jax.sharding import PartitionSpec as P

CORE_SQUARED = 0.01
F32 = jnp.float32
BF16 = jnp.bfloat16
LANES = 128
LANE_BITS = 7
DEPTH = 32
FEATS = 16
EDGES = 5
INNER = LANES - EDGES
EPIECE = 2
AXES = ("row", "col")


def iota(shape, dim):
    return lax.broadcasted_iota(jnp.int32, shape, dim)


def three_parts(value):
    first = value.astype(BF16)
    rest = value - first.astype(F32)
    second = rest.astype(BF16)
    third = (rest - second.astype(F32)).astype(BF16)
    return (first, second, third)


def dot(left, right):
    return jnp.dot(left, right, preferred_element_type=F32)


def pick(onehot, value):
    first, second, third = three_parts(value)
    return dot(onehot, first) + dot(onehot, second) + dot(onehot, third)


def as_columns(row):
    return jnp.transpose(jnp.broadcast_to(row.astype(F32), (LANES, row.shape[1])))


def shifted(value, steps):
    return pltpu.roll(value, (-steps) % LANES, 1)


def five_taps(far_left, left, here, right, far_right):
    return (far_left + far_right + 4.0 * (left + right) + 6.0 * here) * 0.0625


def cross(left_vec, right_vec):
    return [
        left_vec[1] * right_vec[2] - left_vec[2] * right_vec[1],
        left_vec[2] * right_vec[0] - left_vec[0] * right_vec[2],
        left_vec[0] * right_vec[1] - left_vec[1] * right_vec[0],
    ]


def source_rows(here, ahead):
    segment = [a - h for a, h in zip(ahead, here)]
    centre = [0.5 * (a + h) for a, h in zip(ahead, here)]
    near = []
    for value in centre:
        one, two, three = [part.astype(F32) for part in three_parts(value)]
        near += [one, two, three, one, two, one]
    norm = centre[0] * centre[0] + centre[1] * centre[1] + centre[2] * centre[2]
    near += [part.astype(F32) for part in three_parts(norm)]
    near += [jnp.ones_like(norm)] * 3
    terms = segment + cross(segment, centre)
    tops = [value.astype(BF16).astype(F32) for value in terms]
    sums = tops + [value - top for value, top in zip(terms, tops)]
    return near, sums


def target_rows(targets):
    rows = []
    for value in targets:
        one, two, three = [part.astype(F32) for part in three_parts(-2.0 * value)]
        rows += [one, one, one, two, two, three]
    norm = targets[0] * targets[0] + targets[1] * targets[1] + targets[2] * targets[2]
    rows += [jnp.ones_like(norm)] * 3
    rows += [part.astype(F32) for part in three_parts(norm + CORE_SQUARED)]
    return rows


def pair_sums(start, near, sums, target_side):
    squared = lax.dot_general(
        near, target_side, (((0,), (0,)), ((), ())), preferred_element_type=F32
    )
    root = lax.rsqrt(squared)
    weight = root * root * root
    top = weight.astype(BF16)
    rest = (weight - top.astype(F32)).astype(BF16)
    return start + dot(sums, top) + dot(sums, rest)


def my_place():
    return lax.axis_index("row") * lax.axis_size("col") + lax.axis_index("col")


def target_kernel(pos_hbm, links_hbm, panel_hbm, part_ref, pos_ref, links_ref, panel_ref, sems):
    links_in = pltpu.make_async_copy(links_hbm, links_ref, sems.at[0])
    panel_in = pltpu.make_async_copy(panel_hbm, panel_ref, sems.at[1])
    pos_in = pltpu.make_async_copy(pos_hbm, pos_ref, sems.at[2])
    links_in.start()
    panel_in.start()
    pos_in.start()
    links_in.wait()
    panel_in.wait()
    blocks = pos_ref.shape[1]
    total = links_ref.shape[1]
    base = my_place() * blocks
    mine = pl.ds(pl.multiple_of(base, LANES), blocks)
    lane = iota((blocks, LANES), 1)
    ids = iota((blocks, LANES), 0) + base

    wanted = jnp.concatenate([panel_ref[r : r + 1, :] for r in range(panel_ref.shape[0])], axis=1)
    count = wanted.shape[1]
    wanted_block = lax.shift_right_logical(wanted, LANE_BITS)
    wanted_point = jnp.bitwise_and(wanted, LANES - 1)

    follow_col = as_columns(links_ref[1:2, mine]).astype(jnp.int32)[:, :1]
    found = jnp.zeros((blocks, LANES), F32)
    lane_f = lane.astype(F32)
    for r in range(total // LANES):
        row = links_ref[1:2, r * LANES : (r + 1) * LANES]
        found = found + jnp.where(row == ids, lane_f + float(r * LANES), 0.0)
    precede_col = jnp.sum(found, axis=1, keepdims=True).astype(jnp.int32)

    held_here = wanted_block == (iota((blocks, count), 0) + base)
    before = jnp.logical_and(wanted_point < 2, follow_col == wanted_block)
    after = jnp.logical_and(wanted_point >= LANES - 2, precede_col == wanted_block)
    onehot = jnp.concatenate(
        [
            jnp.where(held_here, 1.0, 0.0).astype(BF16),
            jnp.where(jnp.logical_or(before, after), 1.0, 0.0).astype(BF16),
        ],
        axis=0,
    )

    pos_in.wait()
    stacked = []
    for c in range(3):
        x = pos_ref[c]
        rolled = {s: shifted(x, s) for s in (-2, -1, 1, 2)}
        inner = {
            s: jnp.where((lane >= -s) if s < 0 else (lane < LANES - s), v, 0.0)
            for s, v in rolled.items()
        }
        outer = {s: rolled[s] - inner[s] for s in rolled}
        own = five_taps(inner[-2], inner[-1], x, inner[1], inner[2])
        other = five_taps(outer[-2], outer[-1], 0.0, outer[1], outer[2])
        stacked.append(jnp.transpose(jnp.concatenate([own, other], axis=0)))
    one, two, three = three_parts(jnp.concatenate(stacked, axis=0))
    values = dot(one, onehot) + dot(two, onehot) + dot(three, onehot)
    at_point = iota((LANES, count), 0) == wanted_point
    per = count // LANES
    for c in range(3):
        part = jnp.where(at_point, values[c * LANES : (c + 1) * LANES], 0.0)
        row = jnp.sum(part, axis=0, keepdims=True)
        for i in range(per):
            part_ref[c * per + i : c * per + i + 1, :] = row[:, i * LANES : (i + 1) * LANES]


def owner_links(cap, held, me, links_ref, owner_scr, follow_scr):
    devices = owner_scr.shape[0]
    for r in range(devices):
        owner_scr[r : r + 1, :] = links_ref[0:1, r * LANES : (r + 1) * LANES]
        follow_scr[r : r + 1, :] = links_ref[1:2, r * LANES : (r + 1) * LANES]
    owned = jnp.where(owner_scr[...] == me, 1.0, 0.0)
    upper = jnp.where(iota((LANES, LANES), 0) < iota((LANES, LANES), 1), 1.0, 0.0)
    rank = dot(owned.astype(BF16), upper.astype(BF16))
    follow = follow_scr[...]
    table = jnp.concatenate(
        [
            owned,
            rank,
            lax.shift_right_logical(follow, LANE_BITS).astype(F32),
            jnp.bitwise_and(follow, LANES - 1).astype(F32),
        ],
        axis=1,
    ).astype(BF16)
    cap_shift = cap.bit_length() - 1
    slot = iota((held, devices), 0)
    spread = jnp.where(
        lax.shift_right_logical(slot, cap_shift) == iota((held, devices), 1), 1.0, 0.0
    ).astype(BF16)
    wide = dot(spread, table)
    slots = iota((held, LANES), 0)
    seat = jnp.bitwise_and(slots, cap - 1).astype(F32)
    hit = jnp.logical_and(wide[:, :LANES] == 1.0, wide[:, LANES : 2 * LANES] == seat)
    number = (lax.shift_right_logical(slots, cap_shift) * LANES + iota((held, LANES), 1)).astype(F32)
    target_no = wide[:, 2 * LANES : 3 * LANES] * float(LANES) + wide[:, 3 * LANES :]
    live = jnp.sum(jnp.where(hit, 1.0, 0.0), axis=1, keepdims=True)
    id_col = jnp.sum(jnp.where(hit, number, 0.0), axis=1, keepdims=True) + live - 1.0
    next_col = jnp.sum(jnp.where(hit, target_no, 0.0), axis=1, keepdims=True) + 2.0 * live - 2.0
    id_row = jnp.transpose(jnp.broadcast_to(id_col, (held, LANES)))[:1, :]
    next_row = jnp.transpose(jnp.broadcast_to(next_col, (held, LANES)))[:1, :]
    to_next = jnp.where(next_col == id_row, 1.0, 0.0).astype(BF16)
    to_prev = jnp.where(id_col == next_row, 1.0, 0.0).astype(BF16)
    return to_next, to_prev


def owner_kernel(cap, pos_ref, links_ref, out_ref):
    blocks = pos_ref.shape[1]
    devices = out_ref.shape[0]
    held = devices * cap
    mine = pl.ds(pl.multiple_of(my_place() * blocks, LANES), blocks)
    owner_row = links_ref[0:1, mine]
    owner_col = as_columns(owner_row).astype(jnp.int32)
    same = jnp.logical_and(owner_col == owner_row, iota((blocks, blocks), 0) < iota((blocks, blocks), 1))
    rank = jnp.sum(jnp.where(same, 1.0, 0.0), axis=0, keepdims=True).astype(jnp.int32)
    slot = owner_row * cap + rank
    into = jnp.where(iota((held, blocks), 0) == slot, 1.0, 0.0).astype(BF16)
    placed = pick(into, jnp.concatenate([pos_ref[c] for c in range(3)], axis=1))
    for c in range(3):
        for d in range(devices):
            out_ref[d, c * cap : (c + 1) * cap, :] = placed[
                d * cap : (d + 1) * cap, c * LANES : (c + 1) * LANES
            ]


def source_kernel(cap, pos_ref, links_ref, near_ref, sums_ref, next_ref, prev_ref, owner_scr, follow_scr):
    blocks = pos_ref.shape[1]
    here_all = []
    for c in range(3):
        x = pos_ref[c]
        here_all.append(five_taps(shifted(x, -2), shifted(x, -1), x, shifted(x, 1), shifted(x, 2)))
    ahead_all = [shifted(v, 1) for v in here_all]
    near, sums = source_rows(here_all, ahead_all)
    near += [jnp.zeros_like(near[0])] * (DEPTH - len(near))
    sums += [jnp.zeros_like(sums[0])] * (FEATS - len(sums))
    for rows, out_ref in ((near, near_ref), (sums, sums_ref)):
        by_block = jnp.transpose(jnp.stack(rows), (1, 0, 2)).astype(BF16)
        for b in range(blocks):
            out_ref[:, b * INNER : (b + 1) * INNER] = by_block[b][:, 2 : 2 + INNER]
        tail = out_ref.shape[1] - blocks * INNER
        rest = by_block[0][:, :tail] if out_ref is near_ref else jnp.zeros((FEATS, tail), BF16)
        out_ref[:, blocks * INNER :] = rest
    held = next_ref.shape[0]
    next_ref[...], prev_ref[...] = owner_links(cap, held, my_place(), links_ref, owner_scr, follow_scr)


def pair_kernel(tile, piece, part_ref, near_ref, sums_ref, acc_ref, side_ref, target_ref, rows_scr):
    per = part_ref.shape[0] // 3
    targets = [
        jnp.concatenate([part_ref[c * per + i : c * per + i + 1, :] for i in range(per)], axis=1)
        for c in range(3)
    ]
    rows_scr[...] = jnp.zeros_like(rows_scr)
    for c in range(3):
        target_ref[c : c + 1, :] = targets[c]
    for k, row in enumerate(target_rows(targets)):
        rows_scr[k : k + 1, :] = row
    side_ref[...] = rows_scr[...].astype(BF16)
    count = side_ref.shape[1]

    def one_tile(turn, running):
        for start in range(0, tile, piece):
            size = min(piece, tile - start)
            at = pl.ds(pl.multiple_of(turn * tile + start, LANES), size)
            running = pair_sums(running, near_ref[:, at], sums_ref[:, at], side_ref[...])
        return running

    acc_ref[...] = lax.fori_loop(
        0, near_ref.shape[1] // tile, one_tile, jnp.zeros((FEATS, count), F32)
    )


def held_blocks(cap, arrived_ref, x_scr):
    for c in range(3):
        for d in range(arrived_ref.shape[0]):
            x_scr[c, d * cap : (d + 1) * cap, :] = arrived_ref[d, c * cap : (c + 1) * cap, :]


def pick_rows(rows, onehot):
    filled = jnp.concatenate([rows, jnp.zeros((16 - rows.shape[0], rows.shape[1]), F32)], axis=0)
    parts = dot(jnp.concatenate(three_parts(filled), axis=0), onehot)
    return parts[:16] + parts[16:32] + parts[32:]


def taps_down(rows):
    n = rows.shape[0] - 4
    return five_taps(*[rows[k : k + n] for k in range(5)])


def end_kernel(cap, scale, share, arrived_ref, next_ref, prev_ref, side_ref, target_ref, acc_ref, vel_ref, x_scr, near_scr, sums_scr):
    held_blocks(cap, arrived_ref, x_scr)
    held = x_scr.shape[1]
    turned = [jnp.transpose(x_scr[c]) for c in range(3)]
    after = pick_rows(jnp.concatenate([t[:3] for t in turned], axis=0), prev_ref[...])
    before = pick_rows(jnp.concatenate([t[LANES - 2 :] for t in turned], axis=0), next_ref[...])
    here = []
    ahead = []
    for c in range(3):
        first = taps_down(jnp.concatenate([before[2 * c : 2 * c + 2], turned[c][:5]], axis=0))
        last = taps_down(jnp.concatenate([turned[c][LANES - 5 :], after[3 * c : 3 * c + 3]], axis=0))
        here.append(jnp.concatenate([first[:2], last[:3]], axis=0))
        ahead.append(jnp.concatenate([first[1:], last[1:]], axis=0))
    near, sums = source_rows(here, ahead)
    near_scr[...] = jnp.zeros_like(near_scr)
    sums_scr[...] = jnp.zeros_like(sums_scr)
    for k, value in enumerate(near):
        for e in range(EDGES):
            near_scr[k : k + 1, e * held : (e + 1) * held] = value[e : e + 1, :]
    for k, value in enumerate(sums):
        for e in range(EDGES):
            sums_scr[k : k + 1, e * held : (e + 1) * held] = value[e : e + 1, :]
    acc = acc_ref[...]
    for e in range(0, EDGES * held, EPIECE * held):
        at = slice(e, min(e + EPIECE * held, EDGES * held))
        acc = pair_sums(acc, near_scr[:, at].astype(BF16), sums_scr[:, at].astype(BF16), side_ref[...])
    terms = acc[0:6] + acc[6:12]
    targets = [target_ref[c : c + 1, :] for c in range(3)]
    turned = cross([terms[c : c + 1, :] for c in range(3)], targets)
    velocity = jnp.concatenate(
        [scale * (turned[c] - terms[3 + c : 4 + c, :]) for c in range(3)], axis=0
    )
    group = LANES // share
    for d in range(vel_ref.shape[0]):
        vel_ref[d] = velocity[:, d // group * LANES : (d // group + 1) * LANES]


def smooth_kernel(cap, arrived_ref, next_ref, prev_ref, smooth_ref, x_scr):
    held_blocks(cap, arrived_ref, x_scr)
    held = x_scr.shape[1]
    lane = iota((held, LANES), 1)
    blocks = jnp.concatenate([x_scr[c] for c in range(3)], axis=1)
    around = pick(jnp.concatenate([next_ref[...], prev_ref[...]], axis=0), blocks)
    for c in range(3):
        x = x_scr[c]
        after = around[:held, c * LANES : (c + 1) * LANES]
        before = around[held:, c * LANES : (c + 1) * LANES]
        at = [jnp.where(lane < s, shifted(before, -s), shifted(x, -s)) for s in (2, 1)]
        at.append(x)
        at += [jnp.where(lane >= LANES - s, shifted(after, s), shifted(x, s)) for s in (1, 2)]
        smooth_ref[c] = five_taps(*at)


def swapped(value, axis, steps):
    size = lax.axis_size(axis)
    return [lax.ppermute(value, axis, [(k, k ^ step) for k in range(size)]) for step in steps]


def shards(positions, block_links, panel_points):
    devices = lax.axis_size(AXES)
    blocks = positions.shape[1]
    cap = 2 * blocks // devices
    held = devices * cap
    total = block_links.shape[1]
    points = -(-blocks * INNER // 512) * 512
    panel = panel_points.shape[1]
    count = panel_points.shape[0] * panel
    share = panel // lax.axis_size("col")
    scale = 1.0 / (math.pi * math.sqrt(total * LANES))
    vmem = pl.BlockSpec(memory_space=pltpu.VMEM)
    params = pltpu.CompilerParams(vmem_limit_bytes=40 << 20)
    shape = jax.ShapeDtypeStruct
    rows = 3 * count // LANES

    anywhere = pl.BlockSpec(memory_space=pltpu.HBM)
    part = pl.pallas_call(
        target_kernel,
        out_shape=shape((rows, LANES), F32),
        in_specs=[anywhere] * 3,
        out_specs=vmem,
        scratch_shapes=[
            pltpu.VMEM(positions.shape, F32),
            pltpu.VMEM(block_links.shape, jnp.int32),
            pltpu.VMEM(panel_points.shape, jnp.int32),
            pltpu.SemaphoreType.DMA((3,)),
        ],
        compiler_params=pltpu.CompilerParams(vmem_limit_bytes=32 << 20),
        name="targets",
    )(*[pltpu.with_memory_space_constraint(v, pltpu.HBM) for v in (positions, block_links, panel_points)])
    part, positions, block_links = lax.optimization_barrier((part, positions, block_links))
    outgoing = pl.pallas_call(
        functools.partial(owner_kernel, cap),
        out_shape=shape((devices, 3 * cap, LANES), F32),
        in_specs=[vmem] * 2,
        out_specs=vmem,
        compiler_params=params,
        cost_estimate=pl.CostEstimate(flops=10**9, bytes_accessed=10**6, transcendentals=0),
        name="outgoing",
    )(positions, block_links)
    part = part + swapped(part, "col", [1])[0]
    part, positions, outgoing = lax.optimization_barrier((part, positions, outgoing))
    part = sum(swapped(part, "row", range(1, lax.axis_size("row"))), part)
    near, sums, to_next, to_prev = pl.pallas_call(
        functools.partial(source_kernel, cap),
        out_shape=(
            shape((DEPTH, points), BF16),
            shape((FEATS, points), BF16),
            shape((held, held), BF16),
            shape((held, held), BF16),
        ),
        in_specs=[vmem] * 2,
        out_specs=[vmem] * 4,
        scratch_shapes=[
            pltpu.VMEM((devices, LANES), jnp.int32),
            pltpu.VMEM((devices, LANES), jnp.int32),
        ],
        compiler_params=params,
        cost_estimate=pl.CostEstimate(flops=10**9, bytes_accessed=10**7, transcendentals=0),
        name="sources",
    )(positions, block_links)
    near, part = lax.optimization_barrier((near, part))
    outgoing, part = lax.optimization_barrier((outgoing, part))
    far = swapped(part, "col", range(2, lax.axis_size("col"), 2))
    parts = sum(far, part)
    arrived = lax.all_to_all(outgoing, AXES, split_axis=0, concat_axis=0, tiled=True)
    acc, side, targets = pl.pallas_call(
        functools.partial(pair_kernel, points // 2, 512),
        out_shape=(
            shape((FEATS, count), F32),
            shape((DEPTH, count), BF16),
            shape((3, count), F32),
        ),
        in_specs=[vmem] * 3,
        out_specs=[vmem] * 3,
        scratch_shapes=[pltpu.VMEM((DEPTH, count), F32)],
        compiler_params=params,
        cost_estimate=pl.CostEstimate(
            flops=2 * points * count * 1000, bytes_accessed=10**7, transcendentals=0
        ),
        name="pairs",
    )(parts, near, sums)
    velocity = pl.pallas_call(
        functools.partial(end_kernel, cap, scale, share),
        out_shape=shape((devices, 3, LANES), F32),
        in_specs=[vmem] * 6,
        out_specs=vmem,
        scratch_shapes=[
            pltpu.VMEM((3, held, LANES), F32),
            pltpu.VMEM((DEPTH, EDGES * held), F32),
            pltpu.VMEM((FEATS, EDGES * held), F32),
        ],
        compiler_params=params,
        name="ends",
    )(arrived, to_next, to_prev, side, targets, acc)
    smoothed = pl.pallas_call(
        functools.partial(smooth_kernel, cap),
        out_shape=shape((3, held, LANES), F32),
        in_specs=[vmem] * 3,
        out_specs=vmem,
        scratch_shapes=[pltpu.VMEM((3, held, LANES), F32)],
        compiler_params=params,
        cost_estimate=pl.CostEstimate(flops=10**9, bytes_accessed=10**7, transcendentals=0),
        name="smooth",
    )(arrived, to_next, to_prev)
    shares = lax.all_to_all(velocity, AXES, split_axis=0, concat_axis=0, tiled=True)
    start = my_place() % (LANES // share) * share
    summed = lax.dynamic_slice_in_dim(jnp.sum(shares, axis=0), start, share, 1)
    return (smoothed, summed[None])


def solution(mesh):
    placed = (P(None, AXES, None), P(), P())
    return jax.shard_map(
        shards,
        mesh=mesh,
        in_specs=placed,
        out_specs=(P(None, AXES, None), P("row", None, "col")),
        check_vma=False,
    )
```

```python
import functools
import math

import jax
import jax.numpy as jnp
from jax import lax
from jax.experimental import pallas as pl
from jax.experimental.pallas import tpu as pltpu
from jax.sharding import PartitionSpec as P

CORE_SQUARED = 0.01
F32 = jnp.float32
BF16 = jnp.bfloat16
LANES = 128
LANE_BITS = 7
DEPTH = 32
FEATS = 16
EDGES = 5
INNER = LANES - EDGES
EPIECE = 2
AXES = ("row", "col")


def iota(shape, dim):
    return lax.broadcasted_iota(jnp.int32, shape, dim)


def three_parts(value):
    first = value.astype(BF16)
    rest = value - first.astype(F32)
    second = rest.astype(BF16)
    third = (rest - second.astype(F32)).astype(BF16)
    return (first, second, third)


def dot(left, right):
    return jnp.dot(left, right, preferred_element_type=F32)


def pick(onehot, value):
    first, second, third = three_parts(value)
    return dot(onehot, first) + dot(onehot, second) + dot(onehot, third)


def as_columns(row):
    return jnp.transpose(jnp.broadcast_to(row.astype(F32), (LANES, row.shape[1])))


def shifted(value, steps):
    return pltpu.roll(value, (-steps) % LANES, 1)


def five_taps(far_left, left, here, right, far_right):
    return (far_left + far_right + 4.0 * (left + right) + 6.0 * here) * 0.0625


def cross(left_vec, right_vec):
    return [
        left_vec[1] * right_vec[2] - left_vec[2] * right_vec[1],
        left_vec[2] * right_vec[0] - left_vec[0] * right_vec[2],
        left_vec[0] * right_vec[1] - left_vec[1] * right_vec[0],
    ]


def source_rows(here, ahead):
    segment = [a - h for a, h in zip(ahead, here)]
    centre = [0.5 * (a + h) for a, h in zip(ahead, here)]
    near = []
    for value in centre:
        one, two, three = [part.astype(F32) for part in three_parts(value)]
        near += [one, two, three, one, two, one]
    norm = centre[0] * centre[0] + centre[1] * centre[1] + centre[2] * centre[2]
    near += [part.astype(F32) for part in three_parts(norm)]
    near += [jnp.ones_like(norm)] * 3
    terms = segment + cross(segment, centre)
    tops = [value.astype(BF16).astype(F32) for value in terms]
    sums = tops + [value - top for value, top in zip(terms, tops)]
    return near, sums


def target_rows(targets):
    rows = []
    for value in targets:
        one, two, three = [part.astype(F32) for part in three_parts(-2.0 * value)]
        rows += [one, one, one, two, two, three]
    norm = targets[0] * targets[0] + targets[1] * targets[1] + targets[2] * targets[2]
    rows += [jnp.ones_like(norm)] * 3
    rows += [part.astype(F32) for part in three_parts(norm + CORE_SQUARED)]
    return rows


def pair_sums(start, near, sums, target_side):
    squared = lax.dot_general(
        near, target_side, (((0,), (0,)), ((), ())), preferred_element_type=F32
    )
    root = lax.rsqrt(squared)
    weight = root * root * root
    top = weight.astype(BF16)
    rest = (weight - top.astype(F32)).astype(BF16)
    return start + dot(sums, top) + dot(sums, rest)


def my_place():
    return lax.axis_index("row") * lax.axis_size("col") + lax.axis_index("col")


def target_kernel(pos_hbm, links_hbm, panel_hbm, part_ref, pos_ref, links_ref, panel_ref, sems):
    links_in = pltpu.make_async_copy(links_hbm, links_ref, sems.at[0])
    panel_in = pltpu.make_async_copy(panel_hbm, panel_ref, sems.at[1])
    pos_in = pltpu.make_async_copy(pos_hbm, pos_ref, sems.at[2])
    links_in.start()
    panel_in.start()
    pos_in.start()
    links_in.wait()
    panel_in.wait()
    blocks = pos_ref.shape[1]
    total = links_ref.shape[1]
    base = my_place() * blocks
    mine = pl.ds(pl.multiple_of(base, LANES), blocks)
    lane = iota((blocks, LANES), 1)
    ids = iota((blocks, LANES), 0) + base

    wanted = jnp.concatenate([panel_ref[r : r + 1, :] for r in range(panel_ref.shape[0])], axis=1)
    count = wanted.shape[1]
    wanted_block = lax.shift_right_logical(wanted, LANE_BITS)
    wanted_point = jnp.bitwise_and(wanted, LANES - 1)

    follow_col = as_columns(links_ref[1:2, mine]).astype(jnp.int32)[:, :1]
    found = jnp.zeros((blocks, LANES), F32)
    lane_f = lane.astype(F32)
    for r in range(total // LANES):
        row = links_ref[1:2, r * LANES : (r + 1) * LANES]
        found = found + jnp.where(row == ids, lane_f + float(r * LANES), 0.0)
    precede_col = jnp.sum(found, axis=1, keepdims=True).astype(jnp.int32)

    held_here = wanted_block == (iota((blocks, count), 0) + base)
    before = jnp.logical_and(wanted_point < 2, follow_col == wanted_block)
    after = jnp.logical_and(wanted_point >= LANES - 2, precede_col == wanted_block)
    onehot = jnp.concatenate(
        [
            jnp.where(held_here, 1.0, 0.0).astype(BF16),
            jnp.where(jnp.logical_or(before, after), 1.0, 0.0).astype(BF16),
        ],
        axis=0,
    )

    pos_in.wait()
    stacked = []
    for c in range(3):
        x = pos_ref[c]
        rolled = {s: shifted(x, s) for s in (-2, -1, 1, 2)}
        inner = {
            s: jnp.where((lane >= -s) if s < 0 else (lane < LANES - s), v, 0.0)
            for s, v in rolled.items()
        }
        outer = {s: rolled[s] - inner[s] for s in rolled}
        own = five_taps(inner[-2], inner[-1], x, inner[1], inner[2])
        other = five_taps(outer[-2], outer[-1], 0.0, outer[1], outer[2])
        stacked.append(jnp.transpose(jnp.concatenate([own, other], axis=0)))
    one, two, three = three_parts(jnp.concatenate(stacked, axis=0))
    values = dot(one, onehot) + dot(two, onehot) + dot(three, onehot)
    at_point = iota((LANES, count), 0) == wanted_point
    per = count // LANES
    for c in range(3):
        part = jnp.where(at_point, values[c * LANES : (c + 1) * LANES], 0.0)
        row = jnp.sum(part, axis=0, keepdims=True)
        for i in range(per):
            part_ref[c * per + i : c * per + i + 1, :] = row[:, i * LANES : (i + 1) * LANES]


def owner_links(cap, held, me, links_ref, owner_scr, follow_scr):
    devices = owner_scr.shape[0]
    for r in range(devices):
        owner_scr[r : r + 1, :] = links_ref[0:1, r * LANES : (r + 1) * LANES]
        follow_scr[r : r + 1, :] = links_ref[1:2, r * LANES : (r + 1) * LANES]
    owned = jnp.where(owner_scr[...] == me, 1.0, 0.0)
    upper = jnp.where(iota((LANES, LANES), 0) < iota((LANES, LANES), 1), 1.0, 0.0)
    rank = dot(owned.astype(BF16), upper.astype(BF16))
    follow = follow_scr[...]
    table = jnp.concatenate(
        [
            owned,
            rank,
            lax.shift_right_logical(follow, LANE_BITS).astype(F32),
            jnp.bitwise_and(follow, LANES - 1).astype(F32),
        ],
        axis=1,
    ).astype(BF16)
    cap_shift = cap.bit_length() - 1
    slot = iota((held, devices), 0)
    spread = jnp.where(
        lax.shift_right_logical(slot, cap_shift) == iota((held, devices), 1), 1.0, 0.0
    ).astype(BF16)
    wide = dot(spread, table)
    slots = iota((held, LANES), 0)
    seat = jnp.bitwise_and(slots, cap - 1).astype(F32)
    hit = jnp.logical_and(wide[:, :LANES] == 1.0, wide[:, LANES : 2 * LANES] == seat)
    number = (lax.shift_right_logical(slots, cap_shift) * LANES + iota((held, LANES), 1)).astype(F32)
    target_no = wide[:, 2 * LANES : 3 * LANES] * float(LANES) + wide[:, 3 * LANES :]
    live = jnp.sum(jnp.where(hit, 1.0, 0.0), axis=1, keepdims=True)
    id_col = jnp.sum(jnp.where(hit, number, 0.0), axis=1, keepdims=True) + live - 1.0
    next_col = jnp.sum(jnp.where(hit, target_no, 0.0), axis=1, keepdims=True) + 2.0 * live - 2.0
    id_row = jnp.transpose(jnp.broadcast_to(id_col, (held, LANES)))[:1, :]
    next_row = jnp.transpose(jnp.broadcast_to(next_col, (held, LANES)))[:1, :]
    to_next = jnp.where(next_col == id_row, 1.0, 0.0).astype(BF16)
    to_prev = jnp.where(id_col == next_row, 1.0, 0.0).astype(BF16)
    return to_next, to_prev


def owner_kernel(cap, pos_ref, links_ref, out_ref):
    blocks = pos_ref.shape[1]
    devices = out_ref.shape[0]
    held = devices * cap
    mine = pl.ds(pl.multiple_of(my_place() * blocks, LANES), blocks)
    owner_row = links_ref[0:1, mine]
    owner_col = as_columns(owner_row).astype(jnp.int32)
    same = jnp.logical_and(owner_col == owner_row, iota((blocks, blocks), 0) < iota((blocks, blocks), 1))
    rank = jnp.sum(jnp.where(same, 1.0, 0.0), axis=0, keepdims=True).astype(jnp.int32)
    slot = owner_row * cap + rank
    into = jnp.where(iota((held, blocks), 0) == slot, 1.0, 0.0).astype(BF16)
    placed = pick(into, jnp.concatenate([pos_ref[c] for c in range(3)], axis=1))
    for c in range(3):
        for d in range(devices):
            out_ref[d, c * cap : (c + 1) * cap, :] = placed[
                d * cap : (d + 1) * cap, c * LANES : (c + 1) * LANES
            ]


def source_kernel(cap, pos_ref, links_ref, near_ref, sums_ref, next_ref, prev_ref, owner_scr, follow_scr):
    blocks = pos_ref.shape[1]
    here_all = []
    for c in range(3):
        x = pos_ref[c]
        here_all.append(five_taps(shifted(x, -2), shifted(x, -1), x, shifted(x, 1), shifted(x, 2)))
    ahead_all = [shifted(v, 1) for v in here_all]
    near, sums = source_rows(here_all, ahead_all)
    near += [jnp.zeros_like(near[0])] * (DEPTH - len(near))
    sums += [jnp.zeros_like(sums[0])] * (FEATS - len(sums))
    for rows, out_ref in ((near, near_ref), (sums, sums_ref)):
        by_block = jnp.transpose(jnp.stack(rows), (1, 0, 2)).astype(BF16)
        for b in range(blocks):
            out_ref[:, b * INNER : (b + 1) * INNER] = by_block[b][:, 2 : 2 + INNER]
        tail = out_ref.shape[1] - blocks * INNER
        rest = by_block[0][:, :tail] if out_ref is near_ref else jnp.zeros((FEATS, tail), BF16)
        out_ref[:, blocks * INNER :] = rest
    held = next_ref.shape[0]
    next_ref[...], prev_ref[...] = owner_links(cap, held, my_place(), links_ref, owner_scr, follow_scr)


def pair_kernel(tile, piece, part_ref, near_ref, sums_ref, acc_ref, side_ref, target_ref, rows_scr):
    per = part_ref.shape[0] // 3
    targets = [
        jnp.concatenate([part_ref[c * per + i : c * per + i + 1, :] for i in range(per)], axis=1)
        for c in range(3)
    ]
    rows_scr[...] = jnp.zeros_like(rows_scr)
    for c in range(3):
        target_ref[c : c + 1, :] = targets[c]
    for k, row in enumerate(target_rows(targets)):
        rows_scr[k : k + 1, :] = row
    side_ref[...] = rows_scr[...].astype(BF16)
    count = side_ref.shape[1]

    def one_tile(turn, running):
        for start in range(0, tile, piece):
            size = min(piece, tile - start)
            at = pl.ds(pl.multiple_of(turn * tile + start, LANES), size)
            running = pair_sums(running, near_ref[:, at], sums_ref[:, at], side_ref[...])
        return running

    acc_ref[...] = lax.fori_loop(
        0, near_ref.shape[1] // tile, one_tile, jnp.zeros((FEATS, count), F32)
    )


def held_blocks(cap, arrived_ref, x_scr):
    for c in range(3):
        for d in range(arrived_ref.shape[0]):
            x_scr[c, d * cap : (d + 1) * cap, :] = arrived_ref[d, c * cap : (c + 1) * cap, :]


def pick_rows(rows, onehot):
    filled = jnp.concatenate([rows, jnp.zeros((16 - rows.shape[0], rows.shape[1]), F32)], axis=0)
    parts = dot(jnp.concatenate(three_parts(filled), axis=0), onehot)
    return parts[:16] + parts[16:32] + parts[32:]


def taps_down(rows):
    n = rows.shape[0] - 4
    return five_taps(*[rows[k : k + n] for k in range(5)])


def end_kernel(cap, scale, share, arrived_ref, next_ref, prev_ref, side_ref, target_ref, acc_ref, vel_ref, x_scr):
    held_blocks(cap, arrived_ref, x_scr)
    held = x_scr.shape[1]
    turned = [jnp.transpose(x_scr[c]) for c in range(3)]
    after = pick_rows(jnp.concatenate([t[:3] for t in turned], axis=0), prev_ref[...])
    before = pick_rows(jnp.concatenate([t[LANES - 2 :] for t in turned], axis=0), next_ref[...])
    spare = jnp.zeros((8 - EDGES, held), F32)
    here = []
    ahead = []
    for c in range(3):
        first = taps_down(jnp.concatenate([before[2 * c : 2 * c + 2], turned[c][:5]], axis=0))
        last = taps_down(jnp.concatenate([turned[c][LANES - 5 :], after[3 * c : 3 * c + 3]], axis=0))
        here.append(jnp.concatenate([first[:2], last[:3], spare], axis=0))
        ahead.append(jnp.concatenate([first[1:], last[1:], spare], axis=0))
    near, sums = source_rows(here, ahead)
    near += [jnp.zeros_like(near[0])] * (DEPTH - len(near))
    sums += [jnp.zeros_like(sums[0])] * (FEATS - len(sums))
    near, sums = [jnp.transpose(jnp.stack(v), (1, 0, 2)).astype(BF16) for v in (near, sums)]
    acc = acc_ref[...]
    for e in range(0, EDGES, EPIECE):
        edges = range(e, min(e + EPIECE, EDGES))
        acc = pair_sums(
            acc,
            jnp.concatenate([near[k] for k in edges], axis=1),
            jnp.concatenate([sums[k] for k in edges], axis=1),
            side_ref[...],
        )
    terms = acc[0:6] + acc[6:12]
    targets = [target_ref[c : c + 1, :] for c in range(3)]
    turned = cross([terms[c : c + 1, :] for c in range(3)], targets)
    velocity = jnp.concatenate(
        [scale * (turned[c] - terms[3 + c : 4 + c, :]) for c in range(3)], axis=0
    )
    group = LANES // share
    for d in range(vel_ref.shape[0]):
        vel_ref[d] = velocity[:, d // group * LANES : (d // group + 1) * LANES]


def smooth_kernel(cap, arrived_ref, next_ref, prev_ref, smooth_ref, x_scr):
    held_blocks(cap, arrived_ref, x_scr)
    held = x_scr.shape[1]
    lane = iota((held, LANES), 1)
    blocks = jnp.concatenate([x_scr[c] for c in range(3)], axis=1)
    around = pick(jnp.concatenate([next_ref[...], prev_ref[...]], axis=0), blocks)
    for c in range(3):
        x = x_scr[c]
        after = around[:held, c * LANES : (c + 1) * LANES]
        before = around[held:, c * LANES : (c + 1) * LANES]
        at = [jnp.where(lane < s, shifted(before, -s), shifted(x, -s)) for s in (2, 1)]
        at.append(x)
        at += [jnp.where(lane >= LANES - s, shifted(after, s), shifted(x, s)) for s in (1, 2)]
        smooth_ref[c] = five_taps(*at)


def swapped(value, axis, steps):
    size = lax.axis_size(axis)
    return [lax.ppermute(value, axis, [(k, k ^ step) for k in range(size)]) for step in steps]


def shards(positions, block_links, panel_points):
    devices = lax.axis_size(AXES)
    blocks = positions.shape[1]
    cap = 2 * blocks // devices
    held = devices * cap
    total = block_links.shape[1]
    points = -(-blocks * INNER // 512) * 512
    panel = panel_points.shape[1]
    count = panel_points.shape[0] * panel
    share = panel // lax.axis_size("col")
    scale = 1.0 / (math.pi * math.sqrt(total * LANES))
    vmem = pl.BlockSpec(memory_space=pltpu.VMEM)
    params = pltpu.CompilerParams(vmem_limit_bytes=40 << 20)
    shape = jax.ShapeDtypeStruct
    rows = 3 * count // LANES

    anywhere = pl.BlockSpec(memory_space=pltpu.HBM)
    part = pl.pallas_call(
        target_kernel,
        out_shape=shape((rows, LANES), F32),
        in_specs=[anywhere] * 3,
        out_specs=vmem,
        scratch_shapes=[
            pltpu.VMEM(positions.shape, F32),
            pltpu.VMEM(block_links.shape, jnp.int32),
            pltpu.VMEM(panel_points.shape, jnp.int32),
            pltpu.SemaphoreType.DMA((3,)),
        ],
        compiler_params=pltpu.CompilerParams(vmem_limit_bytes=32 << 20),
        name="targets",
    )(*[pltpu.with_memory_space_constraint(v, pltpu.HBM) for v in (positions, block_links, panel_points)])
    part, positions, block_links = lax.optimization_barrier((part, positions, block_links))
    outgoing = pl.pallas_call(
        functools.partial(owner_kernel, cap),
        out_shape=shape((devices, 3 * cap, LANES), F32),
        in_specs=[vmem] * 2,
        out_specs=vmem,
        compiler_params=params,
        cost_estimate=pl.CostEstimate(flops=10**9, bytes_accessed=10**6, transcendentals=0),
        name="outgoing",
    )(positions, block_links)
    part = part + swapped(part, "col", [1])[0]
    part, positions, outgoing = lax.optimization_barrier((part, positions, outgoing))
    part = sum(swapped(part, "row", range(lax.axis_size("row") - 1, 0, -1)), part)
    near, sums, to_next, to_prev = pl.pallas_call(
        functools.partial(source_kernel, cap),
        out_shape=(
            shape((DEPTH, points), BF16),
            shape((FEATS, points), BF16),
            shape((held, held), BF16),
            shape((held, held), BF16),
        ),
        in_specs=[vmem] * 2,
        out_specs=[vmem] * 4,
        scratch_shapes=[
            pltpu.VMEM((devices, LANES), jnp.int32),
            pltpu.VMEM((devices, LANES), jnp.int32),
        ],
        compiler_params=params,
        cost_estimate=pl.CostEstimate(flops=10**9, bytes_accessed=10**7, transcendentals=0),
        name="sources",
    )(positions, block_links)
    near, part = lax.optimization_barrier((near, part))
    outgoing, part = lax.optimization_barrier((outgoing, part))
    far = swapped(part, "col", range(lax.axis_size("col") - 2, 0, -2))
    parts = sum(far, part)
    arrived = lax.all_to_all(outgoing, AXES, split_axis=0, concat_axis=0, tiled=True)
    acc, side, targets = pl.pallas_call(
        functools.partial(pair_kernel, points // 2, 512),
        out_shape=(
            shape((FEATS, count), F32),
            shape((DEPTH, count), BF16),
            shape((3, count), F32),
        ),
        in_specs=[vmem] * 3,
        out_specs=[vmem] * 3,
        scratch_shapes=[pltpu.VMEM((DEPTH, count), F32)],
        compiler_params=params,
        cost_estimate=pl.CostEstimate(
            flops=2 * points * count * 1000, bytes_accessed=10**7, transcendentals=0
        ),
        name="pairs",
    )(parts, near, sums)
    velocity = pl.pallas_call(
        functools.partial(end_kernel, cap, scale, share),
        out_shape=shape((devices, 3, LANES), F32),
        in_specs=[vmem] * 6,
        out_specs=vmem,
        scratch_shapes=[pltpu.VMEM((3, held, LANES), F32)],
        compiler_params=params,
        name="ends",
    )(arrived, to_next, to_prev, side, targets, acc)
    smoothed = pl.pallas_call(
        functools.partial(smooth_kernel, cap),
        out_shape=shape((3, held, LANES), F32),
        in_specs=[vmem] * 3,
        out_specs=vmem,
        scratch_shapes=[pltpu.VMEM((3, held, LANES), F32)],
        compiler_params=params,
        cost_estimate=pl.CostEstimate(flops=10**9, bytes_accessed=10**7, transcendentals=0),
        name="smooth",
    )(arrived, to_next, to_prev)
    shares = lax.all_to_all(velocity, AXES, split_axis=0, concat_axis=0, tiled=True)
    start = my_place() % (LANES // share) * share
    summed = lax.dynamic_slice_in_dim(jnp.sum(shares, axis=0), start, share, 1)
    return (smoothed, summed[None])


def solution(mesh):
    placed = (P(None, AXES, None), P(), P())
    return jax.shard_map(
        shards,
        mesh=mesh,
        in_specs=placed,
        out_specs=(P(None, AXES, None), P("row", None, "col")),
        check_vma=False,
    )
```

```python
import functools
import math

import jax
import jax.numpy as jnp
from jax import lax
from jax.experimental import pallas as pl
from jax.experimental.pallas import tpu as pltpu
from jax.sharding import PartitionSpec as P

CORE_SQUARED = 0.01
F32 = jnp.float32
BF16 = jnp.bfloat16
LANES = 128
LANE_BITS = 7
DEPTH = 32
FEATS = 16
EDGES = 5
INNER = LANES - EDGES
EPIECE = 2
AXES = ("row", "col")


def iota(shape, dim):
    return lax.broadcasted_iota(jnp.int32, shape, dim)


def three_parts(value):
    first = value.astype(BF16)
    rest = value - first.astype(F32)
    second = rest.astype(BF16)
    third = (rest - second.astype(F32)).astype(BF16)
    return (first, second, third)


def dot(left, right):
    return jnp.dot(left, right, preferred_element_type=F32)


def pick(onehot, value):
    first, second, third = three_parts(value)
    return dot(onehot, first) + dot(onehot, second) + dot(onehot, third)


def as_columns(row):
    return jnp.transpose(jnp.broadcast_to(row.astype(F32), (LANES, row.shape[1])))


def shifted(value, steps):
    return pltpu.roll(value, (-steps) % LANES, 1)


def five_taps(far_left, left, here, right, far_right):
    return (far_left + far_right + 4.0 * (left + right) + 6.0 * here) * 0.0625


def cross(left_vec, right_vec):
    return [
        left_vec[1] * right_vec[2] - left_vec[2] * right_vec[1],
        left_vec[2] * right_vec[0] - left_vec[0] * right_vec[2],
        left_vec[0] * right_vec[1] - left_vec[1] * right_vec[0],
    ]


def source_rows(here, ahead):
    segment = [a - h for a, h in zip(ahead, here)]
    centre = [0.5 * (a + h) for a, h in zip(ahead, here)]
    near = []
    for value in centre:
        one, two, three = [part.astype(F32) for part in three_parts(value)]
        near += [one, two, three, one, two, one]
    norm = centre[0] * centre[0] + centre[1] * centre[1] + centre[2] * centre[2]
    near += [part.astype(F32) for part in three_parts(norm)]
    near += [jnp.ones_like(norm)] * 3
    terms = segment + cross(segment, centre)
    tops = [value.astype(BF16).astype(F32) for value in terms]
    sums = tops + [value - top for value, top in zip(terms, tops)]
    return near, sums


def target_rows(targets):
    rows = []
    for value in targets:
        one, two, three = [part.astype(F32) for part in three_parts(-2.0 * value)]
        rows += [one, one, one, two, two, three]
    norm = targets[0] * targets[0] + targets[1] * targets[1] + targets[2] * targets[2]
    rows += [jnp.ones_like(norm)] * 3
    rows += [part.astype(F32) for part in three_parts(norm + CORE_SQUARED)]
    return rows


def pair_sums(start, near, sums, target_side):
    squared = lax.dot_general(
        near, target_side, (((0,), (0,)), ((), ())), preferred_element_type=F32
    )
    root = lax.rsqrt(squared)
    weight = root * root * root
    top = weight.astype(BF16)
    rest = (weight - top.astype(F32)).astype(BF16)
    return start + dot(sums, top) + dot(sums, rest)


def my_place():
    return lax.axis_index("row") * lax.axis_size("col") + lax.axis_index("col")


def target_kernel(pos_hbm, links_hbm, panel_hbm, part_ref, pos_ref, links_ref, panel_ref, sems):
    links_in = pltpu.make_async_copy(links_hbm, links_ref, sems.at[0])
    panel_in = pltpu.make_async_copy(panel_hbm, panel_ref, sems.at[1])
    pos_in = pltpu.make_async_copy(pos_hbm, pos_ref, sems.at[2])
    links_in.start()
    panel_in.start()
    pos_in.start()
    links_in.wait()
    panel_in.wait()
    blocks = pos_ref.shape[1]
    total = links_ref.shape[1]
    base = my_place() * blocks
    mine = pl.ds(pl.multiple_of(base, LANES), blocks)
    lane = iota((blocks, LANES), 1)
    ids = iota((blocks, LANES), 0) + base

    wanted = jnp.concatenate([panel_ref[r : r + 1, :] for r in range(panel_ref.shape[0])], axis=1)
    count = wanted.shape[1]
    wanted_block = lax.shift_right_logical(wanted, LANE_BITS)
    wanted_point = jnp.bitwise_and(wanted, LANES - 1)

    follow_col = as_columns(links_ref[1:2, mine]).astype(jnp.int32)[:, :1]
    found = jnp.zeros((blocks, LANES), F32)
    lane_f = lane.astype(F32)
    for r in range(total // LANES):
        row = links_ref[1:2, r * LANES : (r + 1) * LANES]
        found = found + jnp.where(row == ids, lane_f + float(r * LANES), 0.0)
    precede_col = jnp.sum(found, axis=1, keepdims=True).astype(jnp.int32)

    held_here = wanted_block == (iota((blocks, count), 0) + base)
    before = jnp.logical_and(wanted_point < 2, follow_col == wanted_block)
    after = jnp.logical_and(wanted_point >= LANES - 2, precede_col == wanted_block)
    onehot = jnp.concatenate(
        [
            jnp.where(held_here, 1.0, 0.0).astype(BF16),
            jnp.where(jnp.logical_or(before, after), 1.0, 0.0).astype(BF16),
        ],
        axis=0,
    )

    pos_in.wait()
    stacked = []
    for c in range(3):
        x = pos_ref[c]
        rolled = {s: shifted(x, s) for s in (-2, -1, 1, 2)}
        inner = {
            s: jnp.where((lane >= -s) if s < 0 else (lane < LANES - s), v, 0.0)
            for s, v in rolled.items()
        }
        outer = {s: rolled[s] - inner[s] for s in rolled}
        own = five_taps(inner[-2], inner[-1], x, inner[1], inner[2])
        other = five_taps(outer[-2], outer[-1], 0.0, outer[1], outer[2])
        stacked.append(jnp.transpose(jnp.concatenate([own, other], axis=0)))
    parts = dot(jnp.concatenate(three_parts(jnp.concatenate(stacked, axis=0)), axis=0), onehot)
    size = 3 * LANES
    values = parts[:size] + parts[size : 2 * size] + parts[2 * size :]
    at_point = iota((LANES, count), 0) == wanted_point
    per = count // LANES
    for c in range(3):
        part = jnp.where(at_point, values[c * LANES : (c + 1) * LANES], 0.0)
        row = jnp.sum(part, axis=0, keepdims=True)
        for i in range(per):
            part_ref[c * per + i : c * per + i + 1, :] = row[:, i * LANES : (i + 1) * LANES]


def owner_links(cap, held, me, links_ref, owner_scr, follow_scr):
    devices = owner_scr.shape[0]
    for r in range(devices):
        owner_scr[r : r + 1, :] = links_ref[0:1, r * LANES : (r + 1) * LANES]
        follow_scr[r : r + 1, :] = links_ref[1:2, r * LANES : (r + 1) * LANES]
    owned = jnp.where(owner_scr[...] == me, 1.0, 0.0)
    upper = jnp.where(iota((LANES, LANES), 0) < iota((LANES, LANES), 1), 1.0, 0.0)
    rank = dot(owned.astype(BF16), upper.astype(BF16))
    follow = follow_scr[...]
    table = jnp.concatenate(
        [
            owned,
            rank,
            lax.shift_right_logical(follow, LANE_BITS).astype(F32),
            jnp.bitwise_and(follow, LANES - 1).astype(F32),
        ],
        axis=1,
    ).astype(BF16)
    cap_shift = cap.bit_length() - 1
    slot = iota((held, devices), 0)
    spread = jnp.where(
        lax.shift_right_logical(slot, cap_shift) == iota((held, devices), 1), 1.0, 0.0
    ).astype(BF16)
    wide = dot(spread, table)
    slots = iota((held, LANES), 0)
    seat = jnp.bitwise_and(slots, cap - 1).astype(F32)
    hit = jnp.logical_and(wide[:, :LANES] == 1.0, wide[:, LANES : 2 * LANES] == seat)
    number = (lax.shift_right_logical(slots, cap_shift) * LANES + iota((held, LANES), 1)).astype(F32)
    target_no = wide[:, 2 * LANES : 3 * LANES] * float(LANES) + wide[:, 3 * LANES :]
    live = jnp.sum(jnp.where(hit, 1.0, 0.0), axis=1, keepdims=True)
    id_col = jnp.sum(jnp.where(hit, number, 0.0), axis=1, keepdims=True) + live - 1.0
    next_col = jnp.sum(jnp.where(hit, target_no, 0.0), axis=1, keepdims=True) + 2.0 * live - 2.0
    id_row = jnp.transpose(jnp.broadcast_to(id_col, (held, LANES)))[:1, :]
    next_row = jnp.transpose(jnp.broadcast_to(next_col, (held, LANES)))[:1, :]
    to_next = jnp.where(next_col == id_row, 1.0, 0.0).astype(BF16)
    to_prev = jnp.where(id_col == next_row, 1.0, 0.0).astype(BF16)
    return to_next, to_prev


def owner_kernel(cap, pos_ref, links_ref, out_ref):
    blocks = pos_ref.shape[1]
    devices = out_ref.shape[0]
    held = devices * cap
    mine = pl.ds(pl.multiple_of(my_place() * blocks, LANES), blocks)
    owner_row = links_ref[0:1, mine]
    owner_col = as_columns(owner_row).astype(jnp.int32)
    same = jnp.logical_and(owner_col == owner_row, iota((blocks, blocks), 0) < iota((blocks, blocks), 1))
    rank = jnp.sum(jnp.where(same, 1.0, 0.0), axis=0, keepdims=True).astype(jnp.int32)
    slot = owner_row * cap + rank
    into = jnp.where(iota((held, blocks), 0) == slot, 1.0, 0.0).astype(BF16)
    placed = pick(into, jnp.concatenate([pos_ref[c] for c in range(3)], axis=1))
    for c in range(3):
        for d in range(devices):
            out_ref[d, c * cap : (c + 1) * cap, :] = placed[
                d * cap : (d + 1) * cap, c * LANES : (c + 1) * LANES
            ]


def source_kernel(cap, pos_ref, links_ref, near_ref, sums_ref, next_ref, prev_ref, owner_scr, follow_scr):
    blocks = pos_ref.shape[1]
    here_all = []
    for c in range(3):
        x = pos_ref[c]
        here_all.append(five_taps(shifted(x, -2), shifted(x, -1), x, shifted(x, 1), shifted(x, 2)))
    ahead_all = [shifted(v, 1) for v in here_all]
    near, sums = source_rows(here_all, ahead_all)
    near += [jnp.zeros_like(near[0])] * (DEPTH - len(near))
    sums += [jnp.zeros_like(sums[0])] * (FEATS - len(sums))
    for rows, out_ref in ((near, near_ref), (sums, sums_ref)):
        by_block = jnp.transpose(jnp.stack(rows), (1, 0, 2)).astype(BF16)
        for b in range(blocks):
            out_ref[:, b * INNER : (b + 1) * INNER] = by_block[b][:, 2 : 2 + INNER]
        tail = out_ref.shape[1] - blocks * INNER
        rest = by_block[0][:, :tail] if out_ref is near_ref else jnp.zeros((FEATS, tail), BF16)
        out_ref[:, blocks * INNER :] = rest
    held = next_ref.shape[0]
    next_ref[...], prev_ref[...] = owner_links(cap, held, my_place(), links_ref, owner_scr, follow_scr)


def pair_kernel(tile, piece, part_ref, near_ref, sums_ref, acc_ref, side_ref, target_ref, rows_scr):
    per = part_ref.shape[0] // 3
    targets = [
        jnp.concatenate([part_ref[c * per + i : c * per + i + 1, :] for i in range(per)], axis=1)
        for c in range(3)
    ]
    rows_scr[...] = jnp.zeros_like(rows_scr)
    for c in range(3):
        target_ref[c : c + 1, :] = targets[c]
    for k, row in enumerate(target_rows(targets)):
        rows_scr[k : k + 1, :] = row
    side_ref[...] = rows_scr[...].astype(BF16)
    count = side_ref.shape[1]

    def one_tile(turn, running):
        for start in range(0, tile, piece):
            size = min(piece, tile - start)
            at = pl.ds(pl.multiple_of(turn * tile + start, LANES), size)
            running = pair_sums(running, near_ref[:, at], sums_ref[:, at], side_ref[...])
        return running

    acc_ref[...] = lax.fori_loop(
        0, near_ref.shape[1] // tile, one_tile, jnp.zeros((FEATS, count), F32)
    )


def held_blocks(cap, arrived_ref, x_scr):
    for c in range(3):
        for d in range(arrived_ref.shape[0]):
            x_scr[c, d * cap : (d + 1) * cap, :] = arrived_ref[d, c * cap : (c + 1) * cap, :]


def pick_rows(rows, onehot):
    filled = jnp.concatenate([rows, jnp.zeros((16 - rows.shape[0], rows.shape[1]), F32)], axis=0)
    parts = dot(jnp.concatenate(three_parts(filled), axis=0), onehot)
    return parts[:16] + parts[16:32] + parts[32:]


def taps_down(rows):
    n = rows.shape[0] - 4
    return five_taps(*[rows[k : k + n] for k in range(5)])


def end_kernel(cap, scale, share, arrived_ref, next_ref, prev_ref, side_ref, target_ref, acc_ref, vel_ref, x_scr):
    held_blocks(cap, arrived_ref, x_scr)
    held = x_scr.shape[1]
    turned = [jnp.transpose(x_scr[c]) for c in range(3)]
    after = pick_rows(jnp.concatenate([t[:3] for t in turned], axis=0), prev_ref[...])
    before = pick_rows(jnp.concatenate([t[LANES - 2 :] for t in turned], axis=0), next_ref[...])
    spare = jnp.zeros((8 - EDGES, held), F32)
    here = []
    ahead = []
    for c in range(3):
        first = taps_down(jnp.concatenate([before[2 * c : 2 * c + 2], turned[c][:5]], axis=0))
        last = taps_down(jnp.concatenate([turned[c][LANES - 5 :], after[3 * c : 3 * c + 3]], axis=0))
        here.append(jnp.concatenate([first[:2], last[:3], spare], axis=0))
        ahead.append(jnp.concatenate([first[1:], last[1:], spare], axis=0))
    near, sums = source_rows(here, ahead)
    near += [jnp.zeros_like(near[0])] * (DEPTH - len(near))
    sums += [jnp.zeros_like(sums[0])] * (FEATS - len(sums))
    near, sums = [jnp.transpose(jnp.stack(v), (1, 0, 2)).astype(BF16) for v in (near, sums)]
    acc = acc_ref[...]
    for e in range(0, EDGES, EPIECE):
        edges = range(e, min(e + EPIECE, EDGES))
        acc = pair_sums(
            acc,
            jnp.concatenate([near[k] for k in edges], axis=1),
            jnp.concatenate([sums[k] for k in edges], axis=1),
            side_ref[...],
        )
    terms = acc[0:6] + acc[6:12]
    targets = [target_ref[c : c + 1, :] for c in range(3)]
    turned = cross([terms[c : c + 1, :] for c in range(3)], targets)
    velocity = jnp.concatenate(
        [scale * (turned[c] - terms[3 + c : 4 + c, :]) for c in range(3)], axis=0
    )
    group = LANES // share
    for d in range(vel_ref.shape[0]):
        vel_ref[d] = velocity[:, d // group * LANES : (d // group + 1) * LANES]


def smooth_kernel(cap, arrived_ref, next_ref, prev_ref, smooth_ref, x_scr):
    held_blocks(cap, arrived_ref, x_scr)
    held = x_scr.shape[1]
    lane = iota((held, LANES), 1)
    blocks = jnp.concatenate([x_scr[c] for c in range(3)], axis=1)
    around = pick(jnp.concatenate([next_ref[...], prev_ref[...]], axis=0), blocks)
    for c in range(3):
        x = x_scr[c]
        after = around[:held, c * LANES : (c + 1) * LANES]
        before = around[held:, c * LANES : (c + 1) * LANES]
        at = [jnp.where(lane < s, shifted(before, -s), shifted(x, -s)) for s in (2, 1)]
        at.append(x)
        at += [jnp.where(lane >= LANES - s, shifted(after, s), shifted(x, s)) for s in (1, 2)]
        smooth_ref[c] = five_taps(*at)


def swapped(value, axis, steps):
    size = lax.axis_size(axis)
    return [lax.ppermute(value, axis, [(k, k ^ step) for k in range(size)]) for step in steps]


def shards(positions, block_links, panel_points):
    devices = lax.axis_size(AXES)
    blocks = positions.shape[1]
    cap = 2 * blocks // devices
    held = devices * cap
    total = block_links.shape[1]
    points = -(-blocks * INNER // 512) * 512
    panel = panel_points.shape[1]
    count = panel_points.shape[0] * panel
    share = panel // lax.axis_size("col")
    scale = 1.0 / (math.pi * math.sqrt(total * LANES))
    vmem = pl.BlockSpec(memory_space=pltpu.VMEM)
    params = pltpu.CompilerParams(vmem_limit_bytes=40 << 20)
    shape = jax.ShapeDtypeStruct
    rows = 3 * count // LANES

    anywhere = pl.BlockSpec(memory_space=pltpu.HBM)
    part = pl.pallas_call(
        target_kernel,
        out_shape=shape((rows, LANES), F32),
        in_specs=[anywhere] * 3,
        out_specs=vmem,
        scratch_shapes=[
            pltpu.VMEM(positions.shape, F32),
            pltpu.VMEM(block_links.shape, jnp.int32),
            pltpu.VMEM(panel_points.shape, jnp.int32),
            pltpu.SemaphoreType.DMA((3,)),
        ],
        compiler_params=pltpu.CompilerParams(vmem_limit_bytes=32 << 20),
        name="targets",
    )(*[pltpu.with_memory_space_constraint(v, pltpu.HBM) for v in (positions, block_links, panel_points)])
    part, positions, block_links = lax.optimization_barrier((part, positions, block_links))
    outgoing = pl.pallas_call(
        functools.partial(owner_kernel, cap),
        out_shape=shape((devices, 3 * cap, LANES), F32),
        in_specs=[vmem] * 2,
        out_specs=vmem,
        compiler_params=params,
        cost_estimate=pl.CostEstimate(flops=10**9, bytes_accessed=10**6, transcendentals=0),
        name="outgoing",
    )(positions, block_links)
    part = part + swapped(part, "col", [1])[0]
    part, positions, outgoing = lax.optimization_barrier((part, positions, outgoing))
    part = sum(swapped(part, "row", range(lax.axis_size("row") - 1, 0, -1)), part)
    near, sums, to_next, to_prev = pl.pallas_call(
        functools.partial(source_kernel, cap),
        out_shape=(
            shape((DEPTH, points), BF16),
            shape((FEATS, points), BF16),
            shape((held, held), BF16),
            shape((held, held), BF16),
        ),
        in_specs=[vmem] * 2,
        out_specs=[vmem] * 4,
        scratch_shapes=[
            pltpu.VMEM((devices, LANES), jnp.int32),
            pltpu.VMEM((devices, LANES), jnp.int32),
        ],
        compiler_params=params,
        cost_estimate=pl.CostEstimate(flops=10**9, bytes_accessed=10**7, transcendentals=0),
        name="sources",
    )(positions, block_links)
    near, part = lax.optimization_barrier((near, part))
    outgoing, part = lax.optimization_barrier((outgoing, part))
    far = swapped(part, "col", range(lax.axis_size("col") - 2, 0, -2))
    parts = sum(far, part)
    arrived = lax.all_to_all(outgoing, AXES, split_axis=0, concat_axis=0, tiled=True)
    acc, side, targets = pl.pallas_call(
        functools.partial(pair_kernel, points // 2, 512),
        out_shape=(
            shape((FEATS, count), F32),
            shape((DEPTH, count), BF16),
            shape((3, count), F32),
        ),
        in_specs=[vmem] * 3,
        out_specs=[vmem] * 3,
        scratch_shapes=[pltpu.VMEM((DEPTH, count), F32)],
        compiler_params=params,
        cost_estimate=pl.CostEstimate(
            flops=2 * points * count * 1000, bytes_accessed=10**7, transcendentals=0
        ),
        name="pairs",
    )(parts, near, sums)
    velocity = pl.pallas_call(
        functools.partial(end_kernel, cap, scale, share),
        out_shape=shape((devices, 3, LANES), F32),
        in_specs=[vmem] * 6,
        out_specs=vmem,
        scratch_shapes=[pltpu.VMEM((3, held, LANES), F32)],
        compiler_params=params,
        name="ends",
    )(arrived, to_next, to_prev, side, targets, acc)
    smoothed = pl.pallas_call(
        functools.partial(smooth_kernel, cap),
        out_shape=shape((3, held, LANES), F32),
        in_specs=[vmem] * 3,
        out_specs=vmem,
        scratch_shapes=[pltpu.VMEM((3, held, LANES), F32)],
        compiler_params=params,
        cost_estimate=pl.CostEstimate(flops=10**9, bytes_accessed=10**7, transcendentals=0),
        name="smooth",
    )(arrived, to_next, to_prev)
    shares = lax.all_to_all(velocity, AXES, split_axis=0, concat_axis=0, tiled=True)
    start = my_place() % (LANES // share) * share
    summed = lax.dynamic_slice_in_dim(jnp.sum(shares, axis=0), start, share, 1)
    return (smoothed, summed[None])


def solution(mesh):
    placed = (P(None, AXES, None), P(), P())
    return jax.shard_map(
        shards,
        mesh=mesh,
        in_specs=placed,
        out_specs=(P(None, AXES, None), P("row", None, "col")),
        check_vma=False,
    )
```
